512 devices in a mesh: wide: 64 (over z, x), narrow: 8 (over y, core).
Axes of the slice: x: 4, y: 4, z: 16, core: 2. Of those that a mesh axis runs over, the one named last changes fastest.
Arguments:
- points: bfloat16 [98304, 1024], P('wide')
- coarse_ids: int32 [64], P('wide'), may hold values from 0 to 15
- lists: int32 [16, 2048], replicated, may hold values from 0 to 8191, as said below
- owner_map: int32 [8192], replicated, may hold values from 0 to 8191, as said below
- centroids: bfloat16 [8192, 1024], P('wide'), may hold values from -0.1875 to 0.1875
Outputs:
- new_table: float32 [8192, 1024], P('wide')
- masses: float32 [8192], P('wide')
The draws below stay inside these ranges and needn't reach their ends.
Inputs may be any that keep to these rules, and one draw needn't show every extreme that they name: owner_map is a permutation: the storage row of each centroid; storage row r is held by owner r // 128. `lists`: ids in a row are distinct; in each aligned block of 256 entries of a row, at most 8 ids have storage rows of any one owner, and some owner has exactly 8.
All inputs are finite; a program needn't handle non-finite values.
Results may differ from the reference program's by a relative error of at most 0.0075.
Values may be sent and summed in bfloat16 or wider, within the bound.
No kernel may reach another device: no remote copies, remote signals or barrier semaphores. Data moves between devices by JAX's collectives and lax.ppermute only.
A program may use at most 64 MiB of HBM per device.

```python
import jax
import jax.numpy as jnp
from jax import lax

D = 1024
LIST = 2048
PTS = 1536
NCOARSE = 16
LDEV = 256
CAP = 8
CEN_DEV = 128
CENTROIDS = 8192
POINT_ROWS_TOTAL = 98304
N_WIDE = 64


def layout_tables(key):
    base = jax.random.fold_in(key, 7)
    kperm, kblock = jax.random.split(base, 2)
    owners = CENTROIDS // CEN_DEV
    storage = jax.random.permutation(kperm, CENTROIDS).astype(jnp.int32)
    inverse = jnp.argsort(storage, stable=True).astype(jnp.int32)
    blocks = LIST // LDEV

    def one_block(bkey, column):
        kidx, kforce = jax.random.split(bkey, 2)
        picks = jax.random.permutation(kidx, owners * CAP).astype(jnp.int32)
        forced = jax.random.randint(kforce, (), 0, owners)
        order_key = jnp.where(picks // CAP == forced, 0, 1).astype(jnp.int32)
        order = jnp.argsort(order_key, stable=True)
        chosen = picks[order][:LDEV]
        owner = chosen // CAP
        within = chosen % CAP
        return (owner, within)

    def one_cluster(ckey):
        kshift, kcols = jax.random.split(ckey, 2)
        shifts = jax.random.randint(kshift, (owners,), 0, CEN_DEV)
        col_keys = jax.random.split(kcols, blocks)
        columns = jnp.arange(blocks, dtype=jnp.int32)
        owner, within = jax.vmap(one_block)(col_keys, columns)
        inner = (columns[:, None] * CAP + within + shifts[owner]) % CEN_DEV
        row = owner * CEN_DEV + inner
        return inverse[row.reshape(-1)]
    cluster_keys = jax.random.split(kblock, NCOARSE)
    listed = jax.vmap(one_cluster)(cluster_keys)
    return (listed.astype(jnp.int32), storage)


def draw_lists(key, part):
    listed, storage = layout_tables(key)
    return listed


def draw_owner_map(key, part):
    listed, storage = layout_tables(key)
    return storage


def draw_points(key, part):
    noise_seed_key, scale_seed_key = jax.random.split(jax.random.fold_in(key, 11), 2)
    noise = jax.random.normal(noise_seed_key, (POINT_ROWS_TOTAL, D), jnp.float32)
    scale_factor = jnp.exp(jax.random.uniform(scale_seed_key, (POINT_ROWS_TOTAL, 1), jnp.float32, 0.0, 1.1))
    return (noise * scale_factor * D ** (-0.5)).astype(jnp.bfloat16)


def place_ends(drawn, rng, least, largest):
    spot = [jax.random.randint(jax.random.fold_in(rng, axis), (), 0, length) for axis, length in enumerate(drawn.shape)]
    widest = drawn.shape.index(max(drawn.shape))
    next_to = spot[:widest] + [(spot[widest] + 1) % drawn.shape[widest]] + spot[widest + 1:]
    return drawn.at[tuple(spot)].set(least).at[tuple(next_to)].set(largest)


def level_of(rng, shape, cuts, least, high):
    factor_of, own = 1.0, jax.random.fold_in(rng, 6)
    for axis_at, parts in cuts:
        heights = jnp.exp(jax.random.uniform(jax.random.fold_in(own, axis_at), (parts,), jnp.float32, least / len(cuts), high / len(cuts)))
        factor_of = factor_of * jnp.repeat(heights, shape[axis_at] // parts).reshape([-1 if axis == axis_at else 1 for axis in range(len(shape))])
    return factor_of


def centred(own_key, extent, scale, reach, cuts=(), held_as=jnp.bfloat16):
    factor_of = level_of(own_key, extent, cuts, -0.22, 0.18) if cuts else 1.0
    result = jax.random.normal(own_key, extent, jnp.float32) * scale * factor_of
    return jnp.minimum(jnp.maximum(result, -reach), reach).astype(held_as)


def setup_inputs(seed: int = 0) -> dict:
    seeds = jax.random.split(jax.random.key(seed), 6)
    points = draw_points(jax.random.fold_in(seeds[5], 71), 0)
    coarse_ids = place_ends(jax.random.randint(seeds[1], (N_WIDE,), 0, NCOARSE), jax.random.fold_in(seeds[1], 1), 0, NCOARSE - 1).astype(jnp.int32)
    lists = draw_lists(jax.random.fold_in(seeds[5], 71), 0)
    owner_map = draw_owner_map(jax.random.fold_in(seeds[5], 71), 0)
    centroids = centred(seeds[4], (CENTROIDS, D), (D ** -0.5), 0.1875, ((0, 64),))
    return dict(points=points, coarse_ids=coarse_ids, lists=lists, owner_map=owner_map, centroids=centroids)


temper = 0.1
prior = 0.01


def reference(points, coarse_ids, lists, owner_map, centroids):
    slabs = points.reshape(N_WIDE, PTS, D)

    def one_slab(carry, item):
        totals, weight = carry
        slab, cluster = item
        listed = lax.dynamic_index_in_dim(lists, cluster, 0, keepdims=False)
        stored = owner_map[listed]
        means = centroids[stored]
        norms = jnp.sum(means.astype(jnp.float32) ** 2, axis=1)
        dots = jnp.dot(slab, means.T, preferred_element_type=jnp.float32)
        scores = (2.0 * dots - norms[None, :]) / temper
        top = jnp.max(scores, axis=1, keepdims=True)
        expo = jnp.exp(scores - top)
        resp = (expo / jnp.sum(expo, axis=1, keepdims=True)).astype(jnp.bfloat16)
        sums = jnp.dot(resp.T, slab, preferred_element_type=jnp.float32).astype(jnp.bfloat16)
        mass = jnp.sum(resp.astype(jnp.float32), axis=0).astype(jnp.bfloat16)
        totals = totals.at[stored].add(sums.astype(jnp.float32))
        weight = weight.at[stored].add(mass.astype(jnp.float32))
        return (totals, weight), None

    start = (jnp.zeros((CENTROIDS, D), jnp.float32), jnp.zeros((CENTROIDS,), jnp.float32))
    (totals, weight), _ = lax.scan(one_slab, start, (slabs, coarse_ids))
    new_table = (totals + prior * centroids.astype(jnp.float32)) / (weight + prior)[:, None]
    return new_table, weight
```

```python
import functools

import jax
import jax.numpy as jnp
from jax import lax
from jax.experimental import pallas as pl
from jax.experimental.pallas import tpu as pltpu
from jax.sharding import Mesh, PartitionSpec as P

temper = 0.1
prior = 0.01
gone = -3e38
f32 = jnp.float32
bf16 = jnp.bfloat16
i32 = jnp.int32
near = (0, 1, 2, -1)
lane = 128


def vmem(n):
    return [pl.BlockSpec(memory_space=pltpu.VMEM)] * n


def params():
    return pltpu.CompilerParams(vmem_limit_bytes=40 * 1024 * 1024)


def mask_kernel(place_ref, lists_ref, owner_ref, mask_ref):
    cluster, z, x, n = (place_ref[i] for i in range(4))
    ids = lists_ref[pl.ds(cluster, 1), :]
    count = ids.shape[1]
    blocks = owner_ref.shape[0]
    in_block = lax.broadcasted_iota(i32, (lane, count), 0)
    which = (lax.broadcasted_iota(i32, (blocks, count), 0) == (ids >> 7)).astype(bf16)
    here = in_block == (ids & 127)
    rows = owner_ref[...]

    def pick(table):
        found = lax.dot_general(
            table.astype(f32).astype(bf16),
            which,
            (((0,), (0,)), ((), ())),
            preferred_element_type=f32,
        )
        return jnp.sum(jnp.where(here, found, 0.0), axis=0, keepdims=True).astype(i32)

    owner = pick(rows >> 7)
    inner = pick(rows & 127)
    dx = ((owner & 3) - x) & 3
    dz = ((owner >> 2) - z) & 15
    j = dz & 3
    k = jnp.where(j == 3, ((dz + 1) >> 2) & 3, dz >> 2)
    row = ((dx * 4 + j) * 4 + k) * 16 + (inner & 15)
    mine = (inner >> 4) == n
    block = jnp.where(mine, row >> 7, lane)
    left = (in_block == (row & 127)).astype(bf16)
    right = (in_block == block).astype(bf16)
    mask_ref[...] = lax.dot_general(
        left, right, (((1,), (1,)), ((), ())), preferred_element_type=f32
    )


def score_kernel(piece, means_ref, points_ref, mask_ref, expo_ref, stat_ref):
    means = means_ref[...]
    wide = means.astype(f32)
    norms = jnp.sum(wide * wide, axis=1, keepdims=True)
    first = piece * (means.shape[0] // lane)
    listed = jnp.concatenate(
        [mask_ref[:, first + i : first + i + 1] for i in range(means.shape[0] // lane)], axis=0
    )
    bias = jnp.where(listed > 0.5, norms * (-1.0 / temper), gone)
    step = 256

    def body(c, _):
        at = pl.ds(pl.multiple_of(c * step, step), step)
        dots = lax.dot_general(
            means, points_ref[at, :], (((1,), (1,)), ((), ())), preferred_element_type=f32
        )
        t = dots * (2.0 / temper) + bias
        t = jnp.where(listed > 0.5, t, gone)
        top = jnp.max(t, axis=0, keepdims=True)
        expo = jnp.exp(t - top)
        expo_ref[:, at] = expo
        stat_ref[0:1, at] = top
        stat_ref[1:2, at] = jnp.sum(expo, axis=0, keepdims=True)
        return 0

    lax.fori_loop(0, points_ref.shape[0] // step, body, 0)


def sums_kernel(expo_ref, stat_ref, all_ref, points_ref, out_ref):
    tops = all_ref[:, 0, :]
    top = jnp.max(tops, axis=0, keepdims=True)
    total = jnp.sum(all_ref[:, 1, :] * jnp.exp(tops - top), axis=0, keepdims=True)
    scale = jnp.exp(stat_ref[0:1, :] - top) / total
    resp = (expo_ref[...] * scale).astype(bf16)
    width = points_ref.shape[1]
    step = 256
    for c in range(width // step):
        at = slice(c * step, (c + 1) * step)
        out_ref[:, at] = jnp.dot(
            resp, points_ref[:, at], preferred_element_type=f32
        ).astype(bf16)
    mass = jnp.sum(resp.astype(f32), axis=1, keepdims=True)
    lanes = lax.broadcasted_iota(i32, (resp.shape[0], lane), 1)
    out_ref[:, width:] = jnp.where(lanes == 0, mass, 0.0).astype(bf16)


def added(refs, width):
    total = functools.reduce(lambda a, b: a + b, [r[:, :width].astype(f32) for r in refs])
    mass = functools.reduce(lambda a, b: a + b, [r[:, width:].astype(f32) for r in refs])
    return total, mass[:, 0:1] + mass[:, 1:2]


def add_kernel(a, b, c, d, *outs):
    width = a.shape[1] - lane
    total, mass = added((a, b, c, d), width)
    high = mass.astype(bf16).astype(f32)
    lanes = lax.broadcasted_iota(i32, (a.shape[0], lane), 1)
    tail = jnp.where(lanes == 0, high, jnp.where(lanes == 1, mass - high, 0.0)).astype(bf16)
    total = total.astype(bf16)
    rows = a.shape[0] // 4
    for k, out in enumerate(outs):
        out[:, :width] = total[k * rows : (k + 1) * rows]
        out[:, width:] = tail[k * rows : (k + 1) * rows]


def last_kernel(a, b, c, d, cen, out):
    width = cen.shape[1]
    total, mass = added((a, b, c, d), width)
    out[:, :width] = (total + prior * cen[...].astype(f32)) / (mass + prior)
    out[:, width:] = jnp.broadcast_to(mass, (mass.shape[0], lane))


def shifted(a, axis, by):
    n = lax.axis_size(axis)
    return lax.ppermute(a, axis, [(i, (i + by) % n) for i in range(n)])


def call(kernel, outs, args, specs=None, flops=0, moved=0):
    return pl.pallas_call(
        kernel,
        out_shape=outs,
        in_specs=specs or vmem(len(args)),
        out_specs=jax.tree.map(lambda _: pl.BlockSpec(memory_space=pltpu.VMEM), outs),
        compiler_params=params(),
        cost_estimate=pl.CostEstimate(flops=flops, bytes_accessed=moved, transcendentals=0),
    )(*args)


def shards(points, coarse_ids, lists, owner_map, centroids):
    z, x = lax.axis_index("z"), lax.axis_index("x")
    n = lax.axis_index(("y", "c"))
    count, width = points.shape
    held = centroids.shape[0]
    rows = held // lax.axis_size(("y", "c"))
    sds = jax.ShapeDtypeStruct

    own = lax.dynamic_slice(centroids, (n * rows, 0), (rows, width))
    far = [own] + [shifted(own, "z", -4 * k) for k in (1, 2, 3)]
    group = jnp.concatenate(far, axis=0)
    close = [group] + [shifted(group, "z", -d) for d in near[1:]]
    column = jnp.concatenate(close, axis=0)
    pieces = [column] + [shifted(column, "x", -d) for d in near[1:]]

    place = jnp.stack([coarse_ids[0], z, x, n]).astype(i32)
    mask = call(
        mask_kernel,
        sds((lane, lane), f32),
        (place, lists, owner_map.reshape(-1, lane)),
        [pl.BlockSpec(memory_space=pltpu.SMEM)] + vmem(2),
        moved=4 << 20,
    )
    size = column.shape[0]
    flops = 2 * size * count * width
    scored = [
        call(
            functools.partial(score_kernel, i),
            (sds((size, count), f32), sds((2, count), f32)),
            (piece, points, mask),
            flops=flops,
            moved=4 << 20,
        )
        for i, piece in enumerate(pieces)
    ]
    tops = jnp.stack([s[0] for _, s in scored])
    totals = jnp.stack([s[1] for _, s in scored])
    top = jnp.max(tops, axis=0)
    total = jnp.sum(totals * jnp.exp(tops - top), axis=0)
    both = jnp.stack([top, total])
    shared = lax.all_to_all(
        jnp.broadcast_to(both, (lax.axis_size(("y", "c")), 2, count)), ("y", "c"), 0, 0, tiled=True
    )
    padded = width + lane
    back = [None] * 4
    for i in (2, 1, 3, 0):
        expo, stat = scored[i]
        out = call(
            sums_kernel,
            sds((size, padded), bf16),
            (expo, stat, shared, points),
            flops=flops,
            moved=4 << 20,
        )
        back[i] = shifted(out, "x", near[i]) if i else out
    parts = call(add_kernel, tuple(sds((size // 4, padded), bf16) for _ in near), tuple(back))
    back = [parts[0]] + [shifted(parts[i], "z", near[i]) for i in (1, 2, 3)]
    parts = call(add_kernel, tuple(sds((size // 16, padded), bf16) for _ in near), tuple(back))
    back = [parts[0]] + [shifted(parts[k], "z", 4 * k) for k in (1, 2, 3)]
    table = call(last_kernel, sds((rows, padded), f32), tuple(back) + (own,))
    whole = lax.all_gather(table, ("y", "c"), axis=0, tiled=True)
    return whole[:, :width], whole[:, width]


def solution(mesh):
    chips = Mesh(mesh.devices.reshape(16, 4, 4, 2), ("z", "x", "y", "c"))
    wide = ("z", "x")
    return jax.shard_map(
        shards,
        mesh=chips,
        in_specs=(P(wide, None), P(wide), P(), P(), P(wide, None)),
        out_specs=(P(wide, None), P(wide)),
        check_vma=False,
    )
```

```python
import jax
import jax.numpy as jnp
from jax import lax
from jax.experimental import pallas as pl
from jax.experimental.pallas import tpu as pltpu
from jax.sharding import Mesh, PartitionSpec as P

temper = 0.1
prior = 0.01
gone = -3e38
f32 = jnp.float32
bf16 = jnp.bfloat16
i32 = jnp.int32
lane = 128


def vmem(n):
    return [pl.BlockSpec(memory_space=pltpu.VMEM)] * n


def params():
    return pltpu.CompilerParams(vmem_limit_bytes=40 * 1024 * 1024)


def mask_kernel(place_ref, lists_ref, owner_ref, mask_ref):
    cluster, n = place_ref[0], place_ref[1]
    ids = lists_ref[pl.ds(cluster, 1), :]
    count = ids.shape[1]
    blocks = owner_ref.shape[0]
    in_block = lax.broadcasted_iota(i32, (lane, count), 0)
    which = (lax.broadcasted_iota(i32, (blocks, count), 0) == (ids >> 7)).astype(bf16)
    here = in_block == (ids & 127)
    rows = owner_ref[...]

    def pick(table):
        found = lax.dot_general(
            table.astype(f32).astype(bf16),
            which,
            (((0,), (0,)), ((), ())),
            preferred_element_type=f32,
        )
        return jnp.sum(jnp.where(here, found, 0.0), axis=0, keepdims=True).astype(i32)

    owner = pick(rows >> 7)
    inner = pick(rows & 127)
    row = (owner & 3) * 256 + (owner >> 2) * 16 + (inner & 15)
    block = jnp.where((inner >> 4) == n, row >> 7, lane)
    left = (in_block == (row & 127)).astype(bf16)
    right = (in_block == block).astype(bf16)
    mask_ref[...] = lax.dot_general(
        left, right, (((1,), (1,)), ((), ())), preferred_element_type=f32
    )


def turn_kernel(points_ref, turned_ref):
    step = 256
    for c in range(points_ref.shape[0] // step):
        at = slice(c * step, (c + 1) * step)
        turned_ref[:, at] = points_ref[at, :].T


def score_kernel(means_ref, turned_ref, mask_ref, expo_ref, stat_ref):
    rows = means_ref.shape[0]
    step = 256
    biases, listed = [], []
    for p in range(rows // step):
        wide = means_ref[p * step : (p + 1) * step, :].astype(f32)
        norms = jnp.sum(wide * wide, axis=1, keepdims=True)
        first = p * (step // lane)
        mask = jnp.concatenate([mask_ref[:, first + i : first + i + 1] for i in range(step // lane)])
        listed.append(mask > 0.5)
        biases.append(norms * (-1.0 / temper))
    for c in range(turned_ref.shape[1] // step):
        at = slice(c * step, (c + 1) * step)
        tops = []
        for p in range(rows // step):
            here = slice(p * step, (p + 1) * step)
            dots = jnp.dot(means_ref[here, :], turned_ref[:, at], preferred_element_type=f32)
            t = jnp.where(listed[p], dots * (2.0 / temper) + biases[p], gone)
            expo_ref[here, at] = t
            tops.append(jnp.max(t, axis=0, keepdims=True))
        top = jnp.maximum(jnp.maximum(tops[0], tops[1]), jnp.maximum(tops[2], tops[3]))
        total = jnp.zeros_like(top)
        for p in range(rows // step):
            here = slice(p * step, (p + 1) * step)
            expo = jnp.exp(expo_ref[here, at] - top)
            expo_ref[here, at] = expo
            total = total + jnp.sum(expo, axis=0, keepdims=True)
        stat_ref[0:1, at] = top
        stat_ref[1:2, at] = total


def sums_kernel(expo_ref, stat_ref, all_ref, points_ref, out_ref):
    tops = all_ref[:, 0, :]
    top = jnp.max(tops, axis=0, keepdims=True)
    total = jnp.sum(all_ref[:, 1, :] * jnp.exp(tops - top), axis=0, keepdims=True)
    scale = jnp.exp(stat_ref[0:1, :] - top) / total
    width = points_ref.shape[1]
    step = 256
    for p in range(expo_ref.shape[0] // step):
        here = slice(p * step, (p + 1) * step)
        resp = (expo_ref[here, :] * scale).astype(bf16)
        for c in range(width // step):
            at = slice(c * step, (c + 1) * step)
            out_ref[here, at] = jnp.dot(
                resp, points_ref[:, at], preferred_element_type=f32
            ).astype(bf16)
        mass = jnp.sum(resp.astype(f32), axis=1, keepdims=True)
        lanes = lax.broadcasted_iota(i32, (step, lane), 1)
        out_ref[here, width:] = jnp.where(lanes == 0, mass, 0.0).astype(bf16)


def added(ref, width):
    total = ref[0].astype(f32)
    for k in range(1, ref.shape[0]):
        total = total + ref[k].astype(f32)
    return total[:, :width], total[:, width : width + 1] + total[:, width + 1 : width + 2]


def halves(mass):
    high = mass.astype(bf16).astype(f32)
    lanes = lax.broadcasted_iota(i32, (mass.shape[0], lane), 1)
    return jnp.where(lanes == 0, high, jnp.where(lanes == 1, mass - high, 0.0)).astype(bf16)


def add_kernel(ref, out):
    width = ref.shape[2] - lane
    total, mass = added(ref, width)
    out[:, :width] = total.astype(bf16)
    out[:, width:] = halves(mass)


def last_kernel(ref, cen, out):
    width = cen.shape[1]
    total, mass = added(ref, width)
    new = (total + prior * cen[...].astype(f32)) / (mass + prior)
    new = new.astype(bf16)
    tail = halves(mass)
    for k in range(out.shape[0]):
        out[k, :, :width] = new
        out[k, :, width:] = tail


def call(kernel, outs, args, specs=None, flops=0, moved=0):
    return pl.pallas_call(
        kernel,
        out_shape=outs,
        in_specs=specs or vmem(len(args)),
        out_specs=jax.tree.map(lambda _: pl.BlockSpec(memory_space=pltpu.VMEM), outs),
        compiler_params=params(),
        cost_estimate=pl.CostEstimate(flops=flops, bytes_accessed=moved, transcendentals=0),
    )(*args)


def shards(points, coarse_ids, lists, owner_map, centroids):
    narrow = ("y", "c")
    parts = lax.axis_size(narrow)
    zs, xs = lax.axis_size("z"), lax.axis_size("x")
    n = lax.axis_index(narrow)
    count, width = points.shape
    rows = centroids.shape[0] // parts
    size = rows * zs
    padded = width + lane
    sds = jax.ShapeDtypeStruct

    own = lax.dynamic_slice(centroids, (n * rows, 0), (rows, width))
    column = lax.all_gather(own, "z", axis=0, tiled=True)
    copies = jnp.broadcast_to(column, (xs, size, width))
    means = lax.all_to_all(copies, "x", 0, 0, tiled=True).reshape(xs * size, width)

    place = jnp.stack([coarse_ids[0], n]).astype(i32)
    mask = call(
        mask_kernel,
        sds((lane, lane), f32),
        (place, lists, owner_map.reshape(-1, lane)),
        [pl.BlockSpec(memory_space=pltpu.SMEM)] + vmem(2),
        moved=4 << 20,
    )
    turned = call(turn_kernel, sds((width, count), bf16), (points,), moved=8 << 20)
    flops = 2 * xs * size * count * width
    expo, stat = call(
        score_kernel,
        (sds((xs * size, count), f32), sds((2, count), f32)),
        (means, turned, mask),
        flops=flops,
        moved=16 << 20,
    )
    shared = lax.all_to_all(jnp.broadcast_to(stat, (parts, 2, count)), narrow, 0, 0, tiled=True)
    sums = call(
        sums_kernel,
        sds((xs * size, padded), bf16),
        (expo, stat, shared, points),
        flops=flops,
        moved=16 << 20,
    )
    got = lax.all_to_all(sums.reshape(xs, size, padded), "x", 0, 0, tiled=True)
    sums = call(add_kernel, sds((size, padded), bf16), (got,))
    got = lax.all_to_all(sums.reshape(zs, rows, padded), "z", 0, 0, tiled=True)
    table = call(last_kernel, sds((parts, rows, padded), bf16), (got, own))
    whole = lax.all_to_all(table, narrow, 0, 0, tiled=True).reshape(parts * rows, padded).astype(f32)
    return whole[:, :width], whole[:, width] + whole[:, width + 1]


def solution(mesh):
    chips = Mesh(mesh.devices.reshape(16, 4, 4, 2), ("z", "x", "y", "c"))
    wide = ("z", "x")
    return jax.shard_map(
        shards,
        mesh=chips,
        in_specs=(P(wide, None), P(wide), P(), P(), P(wide, None)),
        out_specs=(P(wide, None), P(wide)),
        check_vma=False,
    )
```

```python
import functools

import jax
import jax.numpy as jnp
from jax import lax
from jax.experimental import pallas as pl
from jax.experimental.pallas import tpu as pltpu
from jax.sharding import Mesh, PartitionSpec as P

temper = 0.1
prior = 0.01
gone = -3e38
f32 = jnp.float32
bf16 = jnp.bfloat16
i32 = jnp.int32
lane = 128


def vmem(n):
    return [pl.BlockSpec(memory_space=pltpu.VMEM)] * n


def params():
    return pltpu.CompilerParams(vmem_limit_bytes=20 * 1024 * 1024)


def mask_kernel(place_ref, other_ref, lists_ref, owner_ref, mask_ref):
    n, x = place_ref[1], place_ref[2]
    count = lists_ref.shape[1]
    blocks = owner_ref.shape[0]
    in_block = lax.broadcasted_iota(i32, (lane, count), 0)
    of_blocks = lax.broadcasted_iota(i32, (blocks, count), 0)
    rows = owner_ref[...]
    tables = [(rows >> 7).astype(f32).astype(bf16), (rows & 127).astype(f32).astype(bf16)]
    mask = jnp.zeros(mask_ref.shape, f32)
    for slab, cluster in enumerate((place_ref[0], other_ref[0])):
        ids = lists_ref[pl.ds(cluster, 1), :]
        which = (of_blocks == (ids >> 7)).astype(bf16)
        here = in_block == (ids & 127)
        owner, inner = (
            jnp.sum(
                jnp.where(
                    here,
                    lax.dot_general(
                        table, which, (((0,), (0,)), ((), ())), preferred_element_type=f32
                    ),
                    0.0,
                ),
                axis=0,
                keepdims=True,
            ).astype(i32)
            for table in tables
        )
        column = owner & 3
        row = (owner >> 2) * 16 + (inner & 15)
        block = (row >> 7) + jnp.where(column == x, 0, 2) + 4 * slab
        mine = ((inner >> 4) == n) & ((column == x) | (column == 3 - x))
        left = (in_block == (row & 127)).astype(bf16)
        right = (in_block == jnp.where(mine, block, lane)).astype(bf16)
        mask = mask + lax.dot_general(
            left, right, (((1,), (1,)), ((), ())), preferred_element_type=f32
        )
    mask_ref[...] = mask


def turn_kernel(*refs):
    turned_ref = refs[-1]
    step = 256
    base = 0
    for points_ref in refs[:-1]:
        for c in range(points_ref.shape[0] // step):
            at = slice(c * step, (c + 1) * step)
            turned_ref[:, base : base + step] = points_ref[at, :].T
            base += step


def squares(means_ref):
    wide = means_ref[...].astype(f32)
    return jnp.sum(wide * wide, axis=1, keepdims=True) * (-1.0 / temper)


def listed_rows(mask_ref, first, rows):
    picked = [mask_ref[:, first + i : first + i + 1] for i in range(rows // lane)]
    return jnp.concatenate(picked) > 0.5


def scored(means_ref, turned_ref, bias, listed, at):
    dots = jnp.dot(means_ref[...], turned_ref[:, at], preferred_element_type=f32)
    t = jnp.where(listed, dots * (2.0 / temper) + bias, gone)
    top = jnp.max(t, axis=0, keepdims=True)
    expo = jnp.exp(t - top)
    return expo, top, jnp.sum(expo, axis=0, keepdims=True)


def own_kernel(slab, means_ref, turned_ref, mask_ref, expo_ref, stat_ref):
    bias = squares(means_ref)
    listed = listed_rows(mask_ref, 4 * slab, means_ref.shape[0])
    step = 256
    for c in range(turned_ref.shape[1] // step):
        at = slice(c * step, (c + 1) * step)
        expo_ref[:, at], stat_ref[0:1, at], stat_ref[1:2, at] = scored(
            means_ref, turned_ref, bias, listed, at
        )


def rest_kernel(
    place_ref,
    means_ref,
    turned_a,
    turned_b,
    mask_ref,
    stat_a,
    stat_b,
    expo_a,
    expo_b,
    stat_c,
    stat_d,
    both_ref,
):
    bias = squares(means_ref)
    me, core = place_ref[3], place_ref[4]
    count = turned_a.shape[1]
    step = 256
    half = count // 2
    for slab, turned_ref, old_ref, expo_ref, stat_ref in (
        (0, turned_a, stat_a, expo_a, stat_c),
        (1, turned_b, stat_b, expo_b, stat_d),
    ):
        listed = listed_rows(mask_ref, 4 * slab + 2, means_ref.shape[0])
        for c in range(count // step):
            at = slice(c * step, (c + 1) * step)
            expo_ref[:, at], top, total = scored(means_ref, turned_ref, bias, listed, at)
            stat_ref[0:1, at] = top
            stat_ref[1:2, at] = total
            before = old_ref[0:1, at]
            join = jnp.maximum(top, before)
            total = total * jnp.exp(top - join) + old_ref[1:2, at] * jnp.exp(before - join)
            if slab == 0:
                start, which = c * step, me
            else:
                shift = half * core
                start = c * step + (shift if c * step < half else -shift)
                start, which = pl.multiple_of(start, lane), 1 - me
            both_ref[which, 0:1, pl.ds(start, step)] = join
            both_ref[which, 1:2, pl.ds(start, step)] = total


def sums_kernel(
    place_ref,
    expo_a,
    expo_b,
    stat_a,
    stat_b,
    all_ref,
    points_ref,
    first_ref,
    second_ref,
    out_ref,
    norm_ref,
):
    me, core = place_ref[3], place_ref[4]
    half = first_ref.shape[0]
    width = points_ref.shape[1]
    for slab, which in enumerate((me, 1 - me)):
        tops = all_ref[:, which, 0, :]
        top = jnp.max(tops, axis=0, keepdims=True)
        total = jnp.sum(all_ref[:, which, 1, :] * jnp.exp(tops - top), axis=0, keepdims=True)
        norm_ref[slab, 0:1, :] = top
        norm_ref[slab, 1:2, :] = total

    def shares(expo, stat, top, total):
        return (expo * (jnp.exp(stat - top) / total)).astype(bf16)

    parts = [shares(expo_a[...], stat_a[0:1, :], norm_ref[0, 0:1, :], norm_ref[0, 1:2, :])]
    for h in range(2):
        from_ = pl.ds(pl.multiple_of((core if h == 0 else 1 - core) * half, lane), half)
        at = slice(h * half, (h + 1) * half)
        parts.append(
            shares(
                expo_b[:, at], stat_b[0:1, at], norm_ref[1, 0:1, from_], norm_ref[1, 1:2, from_]
            )
        )
    step = 256
    for c in range(width // step):
        at = slice(c * step, (c + 1) * step)
        total = None
        for part, ref in zip(parts, (points_ref, first_ref, second_ref)):
            more = jnp.dot(part, ref[:, at], preferred_element_type=f32)
            total = more if total is None else total + more
        out_ref[:, at] = total.astype(bf16)
    mass = sum(jnp.sum(part.astype(f32), axis=1, keepdims=True) for part in parts)
    out_ref[:, width:] = halves(mass)


def added(pieces, width):
    total = pieces[0].astype(f32)
    for piece in pieces[1:]:
        total = total + piece.astype(f32)
    return total[:, :width], total[:, width : width + 1] + total[:, width + 1 : width + 2]


def halves(mass):
    high = mass.astype(bf16).astype(f32)
    lanes = lax.broadcasted_iota(i32, (mass.shape[0], lane), 1)
    return jnp.where(lanes == 0, high, jnp.where(lanes == 1, mass - high, 0.0)).astype(bf16)


def add_kernel(a, b, out):
    width = a.shape[1] - lane
    total, mass = added([a[...], b[...]], width)
    out[:, :width] = total.astype(bf16)
    out[:, width:] = halves(mass)


def last_kernel(ref, cen, out):
    width = cen.shape[1]
    total, mass = added([ref[k] for k in range(ref.shape[0])], width)
    new = (total + prior * cen[...].astype(f32)) / (mass + prior)
    new = new.astype(bf16)
    tail = halves(mass)
    for k in range(out.shape[0]):
        out[k, :, :width] = new
        out[k, :, width:] = tail


def call(kernel, outs, args, specs=None, flops=0, moved=0, scratch=()):
    return pl.pallas_call(
        kernel,
        out_shape=outs,
        in_specs=specs or vmem(len(args)),
        out_specs=jax.tree.map(lambda _: pl.BlockSpec(memory_space=pltpu.VMEM), outs),
        scratch_shapes=scratch,
        compiler_params=params(),
        cost_estimate=pl.CostEstimate(flops=flops, bytes_accessed=moved, transcendentals=0),
    )(*args)


def shards(points, coarse_ids, lists, owner_map, centroids):
    narrow = ("y", "c")
    across = ("xh", "xl")
    parts = lax.axis_size(narrow)
    zs = lax.axis_size("z")
    n, x = lax.axis_index(narrow), lax.axis_index(across)
    me, core = lax.axis_index("xl"), lax.axis_index("c")
    count, width = points.shape
    rows = centroids.shape[0] // parts
    size = rows * zs
    padded = width + lane
    sds = jax.ShapeDtypeStruct
    smem = [pl.BlockSpec(memory_space=pltpu.SMEM)]
    swap = [(0, 1), (1, 0)]
    outer = [(0, 3), (3, 0), (1, 2), (2, 1)]

    half = lax.dynamic_slice(points, (core * (count // 2), 0), (count // 2, width))
    first = lax.ppermute(half, "xl", swap)
    other = lax.ppermute(coarse_ids, "xl", swap)
    own = lax.dynamic_slice(centroids, (n * rows, 0), (rows, width))
    column = lax.all_gather(own, "z", axis=0, tiled=True)
    first, other, column = lax.optimization_barrier((first, other, column))
    second = lax.ppermute(first, "c", swap)
    beyond = lax.ppermute(column, across, outer)

    place = jnp.stack([coarse_ids[0], n, x, me, core]).astype(i32)
    mask = call(
        mask_kernel,
        sds((lane, lane), f32),
        (place, other, lists, owner_map.reshape(-1, lane)),
        smem * 2 + vmem(2),
        moved=8 << 20,
    )
    flops = 2 * size * count * width
    turned_a = call(turn_kernel, sds((width, count), bf16), (points,), moved=8 << 20)
    turned_b = call(turn_kernel, sds((width, count), bf16), (first, second), moved=8 << 20)
    expo = sds((size, count), f32)
    stat = sds((2, count), f32)
    (expo_a, stat_a), (expo_b, stat_b) = (
        call(
            functools.partial(own_kernel, slab),
            (expo, stat),
            (column, turned, mask),
            flops=flops,
            moved=6 << 20,
        )
        for slab, turned in enumerate((turned_a, turned_b))
    )
    expo_c, expo_d, stat_c, stat_d, both = call(
        rest_kernel,
        (expo, expo, stat, stat, sds((2, 2, count), f32)),
        (place, beyond, turned_a, turned_b, mask, stat_a, stat_b),
        smem + vmem(6),
        flops=2 * flops,
        moved=12 << 20,
    )
    pool = ("xl",) + narrow
    copies = jnp.broadcast_to(both, (2 * parts, 2, 2, count))
    shared = lax.all_to_all(copies, pool, 0, 0, tiled=True)

    def sums(expo_a, expo_b, stat_a, stat_b):
        return call(
            sums_kernel,
            sds((size, padded), bf16),
            (place, expo_a, expo_b, stat_a, stat_b, shared, points, first, second),
            smem + vmem(8),
            flops=2 * flops,
            moved=10 << 20,
            scratch=[pltpu.VMEM((2, 2, count), f32)],
        )

    away = lax.ppermute(sums(expo_c, expo_d, stat_c, stat_d), across, outer)
    kept = sums(expo_a, expo_b, stat_a, stat_b)
    added_up = call(add_kernel, sds((size, padded), bf16), (kept, away))
    got = lax.all_to_all(added_up.reshape(zs, rows, padded), "z", 0, 0, tiled=True)
    table = call(last_kernel, sds((parts, rows, padded), bf16), (got, own))
    whole = lax.all_to_all(table, narrow, 0, 0, tiled=True).reshape(parts * rows, padded).astype(f32)
    return whole[:, :width], whole[:, width] + whole[:, width + 1]


def solution(mesh):
    chips = Mesh(mesh.devices.reshape(16, 2, 2, 4, 2), ("z", "xh", "xl", "y", "c"))
    wide = ("z", "xh", "xl")
    return jax.shard_map(
        shards,
        mesh=chips,
        in_specs=(P(wide, None), P(wide), P(), P(), P(wide, None)),
        out_specs=(P(wide, None), P(wide)),
        check_vma=False,
    )
```

```python
import functools

import jax
import jax.numpy as jnp
from jax import lax
from jax.experimental import pallas as pl
from jax.experimental.pallas import tpu as pltpu
from jax.sharding import Mesh, PartitionSpec as P

temper = 0.1
prior = 0.01
gone = -3e38
f32 = jnp.float32
bf16 = jnp.bfloat16
i32 = jnp.int32
lane = 128


def vmem(n):
    return [pl.BlockSpec(memory_space=pltpu.VMEM)] * n


def params():
    return pltpu.CompilerParams(vmem_limit_bytes=20 * 1024 * 1024)


def mask_kernel(place_ref, other_ref, lists_ref, owner_ref, mask_ref):
    n, x = place_ref[1], place_ref[2]
    of_lists = lax.broadcasted_iota(i32, lists_ref.shape, 0)
    neighbour = other_ref[0:1, 0:1].astype(f32).astype(i32)
    count = lists_ref.shape[1]
    blocks = owner_ref.shape[0]
    in_block = lax.broadcasted_iota(i32, (lane, count), 0)
    of_blocks = lax.broadcasted_iota(i32, (blocks, count), 0)
    rows = owner_ref[...]
    tables = [(rows >> 7).astype(f32).astype(bf16), (rows & 127).astype(f32).astype(bf16)]
    mask = jnp.zeros(mask_ref.shape, f32)
    for slab, cluster in enumerate((place_ref[0], neighbour)):
        ids = jnp.sum(
            jnp.where(of_lists == cluster, lists_ref[...], 0), axis=0, keepdims=True
        )
        which = (of_blocks == (ids >> 7)).astype(bf16)
        here = in_block == (ids & 127)
        owner, inner = (
            jnp.sum(
                jnp.where(
                    here,
                    lax.dot_general(
                        table, which, (((0,), (0,)), ((), ())), preferred_element_type=f32
                    ),
                    0.0,
                ),
                axis=0,
                keepdims=True,
            ).astype(i32)
            for table in tables
        )
        column = owner & 3
        row = (owner >> 2) * 16 + (inner & 15)
        block = (row >> 7) + jnp.where(column == x, 0, 2) + 4 * slab
        mine = ((inner >> 4) == n) & ((column == x) | (column == 3 - x))
        left = (in_block == (row & 127)).astype(bf16)
        right = (in_block == jnp.where(mine, block, lane)).astype(bf16)
        mask = mask + lax.dot_general(
            left, right, (((1,), (1,)), ((), ())), preferred_element_type=f32
        )
    mask_ref[...] = mask


def cut_kernel(place_ref, points_ref, half_ref, id_ref, sem, id_sem):
    rows = points_ref.shape[0] // 2
    start = pl.multiple_of(place_ref[4] * rows, rows)
    copy = pltpu.make_async_copy(points_ref.at[pl.ds(start, rows)], half_ref.at[pl.ds(0, rows)], sem)
    copy.start()
    id_ref[...] = jnp.full(id_ref.shape, place_ref[0].astype(f32), f32).astype(bf16)
    last = pltpu.make_async_copy(id_ref, half_ref.at[pl.ds(rows, 16)], id_sem)
    last.start()
    last.wait()
    copy.wait()


def squares(means_ref):
    wide = means_ref[...].astype(f32)
    return jnp.sum(wide * wide, axis=1, keepdims=True) * (-1.0 / temper)


def listed_rows(mask_ref, first, rows):
    picked = [mask_ref[:, first + i : first + i + 1] for i in range(rows // lane)]
    return jnp.concatenate(picked) > 0.5


def scored(means_ref, points, bias, listed):
    dots = lax.dot_general(
        means_ref[...], points, (((1,), (1,)), ((), ())), preferred_element_type=f32
    )
    t = jnp.where(listed, dots * (2.0 / temper) + bias, gone)
    top = jnp.max(t, axis=0, keepdims=True)
    expo = jnp.exp(t - top)
    return expo, top, jnp.sum(expo, axis=0, keepdims=True)


def blocks_of(count, *refs):
    step = 256
    rows = count // len(refs)
    for c in range(count // step):
        start = c * step
        ref = refs[start // rows]
        start %= rows
        yield slice(c * step, (c + 1) * step), ref, slice(start, start + step)


def own_kernel(slab, means_ref, mask_ref, *refs):
    *points, expo_ref, stat_ref = refs
    bias = squares(means_ref)
    listed = listed_rows(mask_ref, 4 * slab, means_ref.shape[0])
    for at, ref, rows in blocks_of(expo_ref.shape[1], *points):
        expo_ref[:, at], stat_ref[0:1, at], stat_ref[1:2, at] = scored(
            means_ref, ref[rows, :], bias, listed
        )


def rest_kernel(
    place_ref,
    means_ref,
    points_ref,
    first_ref,
    second_ref,
    mask_ref,
    stat_a,
    stat_b,
    expo_a,
    expo_b,
    stat_c,
    stat_d,
    both_ref,
):
    bias = squares(means_ref)
    me, core = place_ref[3], place_ref[4]
    count = points_ref.shape[0]
    half = count // 2
    for slab, points, old_ref, expo_ref, stat_ref in (
        (0, (points_ref,), stat_a, expo_a, stat_c),
        (1, (first_ref, second_ref), stat_b, expo_b, stat_d),
    ):
        listed = listed_rows(mask_ref, 4 * slab + 2, means_ref.shape[0])
        for at, ref, rows in blocks_of(count, *points):
            expo_ref[:, at], top, total = scored(means_ref, ref[rows, :], bias, listed)
            stat_ref[0:1, at] = top
            stat_ref[1:2, at] = total
            before = old_ref[0:1, at]
            join = jnp.maximum(top, before)
            total = total * jnp.exp(top - join) + old_ref[1:2, at] * jnp.exp(before - join)
            if slab == 0:
                start, which = at.start, me
            else:
                shift = half * core
                start = at.start + (shift if at.start < half else -shift)
                start, which = pl.multiple_of(start, lane), 1 - me
            both_ref[which, 0:1, pl.ds(start, 256)] = join
            both_ref[which, 1:2, pl.ds(start, 256)] = total


def sums_kernel(
    place_ref,
    expo_a,
    expo_b,
    stat_a,
    stat_b,
    all_ref,
    points_ref,
    first_ref,
    second_ref,
    out_ref,
    norm_ref,
):
    me, core = place_ref[3], place_ref[4]
    half = points_ref.shape[0] // 2
    width = points_ref.shape[1]
    for slab, which in enumerate((me, 1 - me)):
        tops = all_ref[:, which, 0, :]
        top = jnp.max(tops, axis=0, keepdims=True)
        total = jnp.sum(all_ref[:, which, 1, :] * jnp.exp(tops - top), axis=0, keepdims=True)
        norm_ref[slab, 0:1, :] = top
        norm_ref[slab, 1:2, :] = total

    def shares(expo, stat, top, total):
        return (expo * (jnp.exp(stat - top) / total)).astype(bf16)

    parts = [shares(expo_a[...], stat_a[0:1, :], norm_ref[0, 0:1, :], norm_ref[0, 1:2, :])]
    for h in range(2):
        from_ = pl.ds(pl.multiple_of((core if h == 0 else 1 - core) * half, lane), half)
        at = slice(h * half, (h + 1) * half)
        parts.append(
            shares(
                expo_b[:, at], stat_b[0:1, at], norm_ref[1, 0:1, from_], norm_ref[1, 1:2, from_]
            )
        )
    step = 256
    for c in range(width // step):
        at = slice(c * step, (c + 1) * step)
        total = None
        for part, ref in zip(parts, (points_ref, first_ref, second_ref)):
            more = jnp.dot(part, ref[: part.shape[1], at], preferred_element_type=f32)
            total = more if total is None else total + more
        out_ref[:, at] = total.astype(bf16)
    mass = sum(jnp.sum(part.astype(f32), axis=1, keepdims=True) for part in parts)
    out_ref[:, width:] = halves(mass)


def added(pieces, width):
    total = pieces[0].astype(f32)
    for piece in pieces[1:]:
        total = total + piece.astype(f32)
    return total[:, :width], total[:, width : width + 1] + total[:, width + 1 : width + 2]


def halves(mass):
    high = mass.astype(bf16).astype(f32)
    lanes = lax.broadcasted_iota(i32, (mass.shape[0], lane), 1)
    return jnp.where(lanes == 0, high, jnp.where(lanes == 1, mass - high, 0.0)).astype(bf16)


def add_kernel(a, b, out):
    width = a.shape[1] - lane
    total, mass = added([a[...], b[...]], width)
    out[:, :width] = total.astype(bf16)
    out[:, width:] = halves(mass)


def last_kernel(ref, cen, out):
    width = cen.shape[1]
    total, mass = added([ref[k] for k in range(ref.shape[0])], width)
    new = (total + prior * cen[...].astype(f32)) / (mass + prior)
    new = new.astype(bf16)
    tail = halves(mass)
    for k in range(out.shape[0]):
        out[k, :, :width] = new
        out[k, :, width:] = tail


def out_kernel(ref, table_ref, mass_ref):
    parts, rows, padded = ref.shape
    width = padded - lane
    tails = []
    for k in range(parts):
        table_ref[k * rows : (k + 1) * rows, :] = ref[k, :, :width].astype(f32)
        tails.append(ref[k, :, width:].astype(f32))
    tail = jnp.concatenate(tails).T
    mass_ref[...] = tail[0:1, :] + tail[1:2, :]


def call(kernel, outs, args, specs=None, flops=0, moved=0, scratch=(), home=pltpu.VMEM):
    return pl.pallas_call(
        kernel,
        out_shape=outs,
        in_specs=specs or vmem(len(args)),
        out_specs=jax.tree.map(lambda _: pl.BlockSpec(memory_space=home), outs),
        scratch_shapes=scratch,
        compiler_params=params(),
        cost_estimate=pl.CostEstimate(flops=flops, bytes_accessed=moved, transcendentals=0),
    )(*args)


def shards(points, coarse_ids, lists, owner_map, centroids):
    narrow = ("y", "c")
    across = ("xh", "xl")
    parts = lax.axis_size(narrow)
    zs = lax.axis_size("z")
    n, x = lax.axis_index(narrow), lax.axis_index(across)
    me, core = lax.axis_index("xl"), lax.axis_index("c")
    count, width = points.shape
    rows = centroids.shape[0] // parts
    size = rows * zs
    padded = width + lane
    sds = jax.ShapeDtypeStruct
    smem = [pl.BlockSpec(memory_space=pltpu.SMEM)]
    swap = [(0, 1), (1, 0)]
    outer = [(0, 3), (3, 0), (1, 2), (2, 1)]

    place = jnp.stack([coarse_ids[0], n, x, me, core]).astype(i32)
    half = call(
        cut_kernel,
        sds((count // 2 + 16, width), bf16),
        (place, points),
        smem + [pl.BlockSpec(memory_space=pltpu.HBM)],
        moved=3 << 20,
        scratch=[
            pltpu.VMEM((16, width), bf16),
            pltpu.SemaphoreType.DMA,
            pltpu.SemaphoreType.DMA,
        ],
        home=pl.ANY,
    )
    first = lax.ppermute(half, "xl", swap)
    own = lax.dynamic_slice(centroids, (n * rows, 0), (rows, width))
    column = lax.all_gather(own, "z", axis=0, tiled=True)
    first, column = lax.optimization_barrier((first, column))
    beyond = lax.ppermute(column, across, outer)
    second = lax.ppermute(first, "c", swap)

    mask = call(
        mask_kernel,
        sds((lane, lane), f32),
        (place, first[count // 2 :, :lane], lists, owner_map.reshape(-1, lane)),
        smem + vmem(3),
        moved=8 << 20,
    )
    flops = 2 * size * count * width
    expo = sds((size, count), f32)
    stat = sds((2, count), f32)
    (expo_a, stat_a), (expo_b, stat_b) = (
        call(
            functools.partial(own_kernel, slab),
            (expo, stat),
            (column, mask) + slabs,
            flops=flops,
            moved=6 << 20,
        )
        for slab, slabs in enumerate(((points,), (first, second)))
    )
    expo_c, expo_d, stat_c, stat_d, both = call(
        rest_kernel,
        (expo, expo, stat, stat, sds((2, 2, count), f32)),
        (place, beyond, points, first, second, mask, stat_a, stat_b),
        smem + vmem(7),
        flops=2 * flops,
        moved=12 << 20,
    )
    pool = ("xl",) + narrow
    copies = jnp.broadcast_to(both, (2 * parts, 2, 2, count))
    shared = lax.all_to_all(copies, pool, 0, 0, tiled=True)

    def sums(expo_a, expo_b, stat_a, stat_b):
        return call(
            sums_kernel,
            sds((size, padded), bf16),
            (place, expo_a, expo_b, stat_a, stat_b, shared, points, first, second),
            smem + vmem(8),
            flops=2 * flops,
            moved=10 << 20,
            scratch=[pltpu.VMEM((2, 2, count), f32)],
        )

    away = lax.ppermute(sums(expo_c, expo_d, stat_c, stat_d), across, outer)
    kept = sums(expo_a, expo_b, stat_a, stat_b)
    added_up = call(add_kernel, sds((size, padded), bf16), (kept, away))
    got = lax.all_to_all(added_up.reshape(zs, rows, padded), "z", 0, 0, tiled=True)
    table = call(last_kernel, sds((parts, rows, padded), bf16), (got, own))
    whole = lax.all_to_all(table, narrow, 0, 0, tiled=True)
    new_table, masses = call(
        out_kernel, (sds((parts * rows, width), f32), sds((1, parts * rows), f32)), (whole,)
    )
    return new_table, masses[0]


def solution(mesh):
    chips = Mesh(mesh.devices.reshape(16, 2, 2, 4, 2), ("z", "xh", "xl", "y", "c"))
    wide = ("z", "xh", "xl")
    return jax.shard_map(
        shards,
        mesh=chips,
        in_specs=(P(wide, None), P(wide), P(), P(), P(wide, None)),
        out_specs=(P(wide, None), P(wide)),
        check_vma=False,
    )
```

```python
import functools

import jax
import jax.numpy as jnp
from jax import lax
from jax.experimental import pallas as pl
from jax.experimental.pallas import tpu as pltpu
from jax.sharding import Mesh, PartitionSpec as P

temper = 0.1
prior = 0.01
gone = -3e38
near = (0, 1, 2, -1)
f32 = jnp.float32
bf16 = jnp.bfloat16
i32 = jnp.int32
lane = 128


def vmem(n):
    return [pl.BlockSpec(memory_space=pltpu.VMEM)] * n


def params():
    return pltpu.CompilerParams(vmem_limit_bytes=20 * 1024 * 1024)


def mask_kernel(place_ref, other_ref, lists_ref, owner_ref, mask_ref):
    n, x = place_ref[1], place_ref[2]
    of_lists = lax.broadcasted_iota(i32, lists_ref.shape, 0)
    neighbour = other_ref[0:1, 0:1].astype(f32).astype(i32)
    count = lists_ref.shape[1]
    blocks = owner_ref.shape[0]
    in_block = lax.broadcasted_iota(i32, (lane, count), 0)
    of_blocks = lax.broadcasted_iota(i32, (blocks, count), 0)
    rows = owner_ref[...]
    tables = [(rows >> 7).astype(f32).astype(bf16), (rows & 127).astype(f32).astype(bf16)]
    mask = jnp.zeros(mask_ref.shape, f32)
    for slab, cluster in enumerate((place_ref[0], neighbour)):
        ids = jnp.sum(
            jnp.where(of_lists == cluster, lists_ref[...], 0), axis=0, keepdims=True
        )
        which = (of_blocks == (ids >> 7)).astype(bf16)
        here = in_block == (ids & 127)
        owner, inner = (
            jnp.sum(
                jnp.where(
                    here,
                    lax.dot_general(
                        table, which, (((0,), (0,)), ((), ())), preferred_element_type=f32
                    ),
                    0.0,
                ),
                axis=0,
                keepdims=True,
            ).astype(i32)
            for table in tables
        )
        column = owner & 3
        row = (owner >> 2) * 16 + (inner & 15)
        block = (row >> 7) + jnp.where(column == x, 0, 2) + 4 * slab
        mine = ((inner >> 4) == n) & ((column == x) | (column == 3 - x))
        left = (in_block == (row & 127)).astype(bf16)
        right = (in_block == jnp.where(mine, block, lane)).astype(bf16)
        mask = mask + lax.dot_general(
            left, right, (((1,), (1,)), ((), ())), preferred_element_type=f32
        )
    mask_ref[...] = mask


def cut_kernel(place_ref, points_ref, half_ref, id_ref, sem, id_sem):
    rows = points_ref.shape[0] // 2
    start = pl.multiple_of(place_ref[4] * rows, rows)
    copy = pltpu.make_async_copy(points_ref.at[pl.ds(start, rows)], half_ref.at[pl.ds(0, rows)], sem)
    copy.start()
    id_ref[...] = jnp.full(id_ref.shape, place_ref[0].astype(f32), f32).astype(bf16)
    last = pltpu.make_async_copy(id_ref, half_ref.at[pl.ds(rows, 16)], id_sem)
    last.start()
    last.wait()
    copy.wait()


def squares(means_ref):
    wide = means_ref[...].astype(f32)
    return jnp.sum(wide * wide, axis=1, keepdims=True) * (-1.0 / temper)


def listed_rows(mask_ref, first, rows):
    picked = [mask_ref[:, first + i : first + i + 1] for i in range(rows // lane)]
    return jnp.concatenate(picked) > 0.5


def scored(means_ref, points, bias, listed):
    dots = lax.dot_general(
        means_ref[...], points, (((1,), (1,)), ((), ())), preferred_element_type=f32
    )
    t = jnp.where(listed, dots * (2.0 / temper) + bias, gone)
    top = jnp.max(t, axis=0, keepdims=True)
    expo = jnp.exp(t - top)
    return expo, top, jnp.sum(expo, axis=0, keepdims=True)


def blocks_of(count, *refs):
    step = 256
    rows = count // len(refs)
    for c in range(count // step):
        start = c * step
        ref = refs[start // rows]
        start %= rows
        yield slice(c * step, (c + 1) * step), ref, slice(start, start + step)


def own_kernel(slab, means_ref, mask_ref, *refs):
    *points, expo_ref, stat_ref = refs
    bias = squares(means_ref)
    listed = listed_rows(mask_ref, 4 * slab, means_ref.shape[0])
    for at, ref, rows in blocks_of(expo_ref.shape[1], *points):
        expo_ref[:, at], stat_ref[0:1, at], stat_ref[1:2, at] = scored(
            means_ref, ref[rows, :], bias, listed
        )


def rest_kernel(
    place_ref,
    means_ref,
    points_ref,
    first_ref,
    second_ref,
    mask_ref,
    stat_a,
    stat_b,
    expo_a,
    expo_b,
    stat_c,
    stat_d,
    both_ref,
):
    bias = squares(means_ref)
    me, core = place_ref[3], place_ref[4]
    count = points_ref.shape[0]
    half = count // 2
    for slab, points, old_ref, expo_ref, stat_ref in (
        (0, (points_ref,), stat_a, expo_a, stat_c),
        (1, (first_ref, second_ref), stat_b, expo_b, stat_d),
    ):
        listed = listed_rows(mask_ref, 4 * slab + 2, means_ref.shape[0])
        for at, ref, rows in blocks_of(count, *points):
            expo_ref[:, at], top, total = scored(means_ref, ref[rows, :], bias, listed)
            stat_ref[0:1, at] = top
            stat_ref[1:2, at] = total
            before = old_ref[0:1, at]
            join = jnp.maximum(top, before)
            total = total * jnp.exp(top - join) + old_ref[1:2, at] * jnp.exp(before - join)
            if slab == 0:
                start, which = at.start, me
            else:
                shift = half * core
                start = at.start + (shift if at.start < half else -shift)
                start, which = pl.multiple_of(start, lane), 1 - me
            both_ref[pl.ds(which, 1), pl.ds(start, 256)] = join + jnp.log(total)


def sums_kernel(
    place_ref,
    expo_a,
    expo_b,
    stat_a,
    stat_b,
    all_ref,
    points_ref,
    first_ref,
    second_ref,
    out_ref,
    norm_ref,
):
    me, core = place_ref[3], place_ref[4]
    half = points_ref.shape[0] // 2
    width = points_ref.shape[1]
    for slab, which in enumerate((me, 1 - me)):
        each = [all_ref[k, pl.ds(which, 1), :] for k in range(all_ref.shape[0])]
        top = functools.reduce(jnp.maximum, each)
        total = functools.reduce(jnp.add, [jnp.exp(one - top) for one in each])
        norm_ref[slab] = top + jnp.log(total)

    def shares(expo, stat, norm):
        return (expo * jnp.exp(stat - norm)).astype(bf16)

    parts = [shares(expo_a[...], stat_a[0:1, :], norm_ref[0])]
    for h in range(2):
        from_ = pl.ds(pl.multiple_of((core if h == 0 else 1 - core) * half, lane), half)
        at = slice(h * half, (h + 1) * half)
        parts.append(shares(expo_b[:, at], stat_b[0:1, at], norm_ref[1, :, from_]))
    step = 256
    for c in range(width // step):
        at = slice(c * step, (c + 1) * step)
        total = None
        for part, ref in zip(parts, (points_ref, first_ref, second_ref)):
            more = jnp.dot(part, ref[: part.shape[1], at], preferred_element_type=f32)
            total = more if total is None else total + more
        out_ref[:, at] = total.astype(bf16)
    mass = sum(jnp.sum(part.astype(f32), axis=1, keepdims=True) for part in parts)
    out_ref[:, width:] = halves(mass)


def added(pieces, width):
    total = pieces[0].astype(f32)
    for piece in pieces[1:]:
        total = total + piece.astype(f32)
    return total[:, :width], total[:, width : width + 1] + total[:, width + 1 : width + 2]


def halves(mass):
    high = mass.astype(bf16).astype(f32)
    lanes = lax.broadcasted_iota(i32, (mass.shape[0], lane), 1)
    return jnp.where(lanes == 0, high, jnp.where(lanes == 1, mass - high, 0.0)).astype(bf16)


def cross_kernel(place_ref, a, b, *rest):
    outs, total_ref = rest[:-1], rest[-1]
    width = a.shape[1] - lane
    total, mass = added([a[...], b[...]], width)
    total_ref[:, :width] = total.astype(bf16)
    total_ref[:, width:] = halves(mass)
    for d, out in zip(near, outs):
        zl = (place_ref[5] + d) & 3
        for zh in range(4):
            at = pl.ds(pl.multiple_of((zh * 4 + zl) * 16, 16), 16)
            out[zh * 16 : (zh + 1) * 16, :] = total_ref[at, :]


def near_kernel(a, b, c, d, out):
    width = a.shape[1] - lane
    total, mass = added([a[...], b[...], c[...], d[...]], width)
    out[:, :width] = total.astype(bf16)
    out[:, width:] = halves(mass)


def last_kernel(ref, cen, out):
    width = cen.shape[1]
    total, mass = added([ref[k] for k in range(ref.shape[0])], width)
    new = (total + prior * cen[...].astype(f32)) / (mass + prior)
    new = new.astype(bf16)
    tail = halves(mass)
    for k in range(out.shape[0]):
        out[k, :, :width] = new
        out[k, :, width:] = tail


def out_kernel(ref, table_ref, mass_ref):
    parts, rows, padded = ref.shape
    width = padded - lane
    tails = []
    for k in range(parts):
        table_ref[k * rows : (k + 1) * rows, :] = ref[k, :, :width].astype(f32)
        tails.append(ref[k, :, width:].astype(f32))
    tail = jnp.concatenate(tails).T
    mass_ref[...] = tail[0:1, :] + tail[1:2, :]


def call(kernel, outs, args, specs=None, flops=0, moved=0, scratch=(), home=pltpu.VMEM):
    return pl.pallas_call(
        kernel,
        out_shape=outs,
        in_specs=specs or vmem(len(args)),
        out_specs=jax.tree.map(lambda _: pl.BlockSpec(memory_space=home), outs),
        scratch_shapes=scratch,
        compiler_params=params(),
        cost_estimate=pl.CostEstimate(flops=flops, bytes_accessed=moved, transcendentals=0),
    )(*args)


def shards(points, coarse_ids, lists, owner_map, centroids):
    narrow = ("y", "c")
    across = ("xh", "xl")
    parts = lax.axis_size(narrow)
    zs = lax.axis_size(("zh", "zl"))
    n, x = lax.axis_index(narrow), lax.axis_index(across)
    me, core = lax.axis_index("xl"), lax.axis_index("c")
    count, width = points.shape
    rows = centroids.shape[0] // parts
    size = rows * zs
    padded = width + lane
    sds = jax.ShapeDtypeStruct
    smem = [pl.BlockSpec(memory_space=pltpu.SMEM)]
    swap = [(0, 1), (1, 0)]
    outer = [(0, 3), (3, 0), (1, 2), (2, 1)]

    place = jnp.stack([coarse_ids[0], n, x, me, core, lax.axis_index("zl")]).astype(i32)
    half = call(
        cut_kernel,
        sds((count // 2 + 16, width), bf16),
        (place, points),
        smem + [pl.BlockSpec(memory_space=pltpu.HBM)],
        moved=3 << 20,
        scratch=[
            pltpu.VMEM((16, width), bf16),
            pltpu.SemaphoreType.DMA,
            pltpu.SemaphoreType.DMA,
        ],
        home=pl.ANY,
    )
    first = lax.ppermute(half, "xl", swap)
    own = lax.dynamic_slice(centroids, (n * rows, 0), (rows, width))
    column = lax.all_gather(own, ("zh", "zl"), axis=0, tiled=True)
    first, column = lax.optimization_barrier((first, column))
    beyond = lax.ppermute(column, across, outer)
    second = lax.ppermute(first, "c", swap)

    mask = call(
        mask_kernel,
        sds((lane, lane), f32),
        (place, first[count // 2 :, :lane], lists, owner_map.reshape(-1, lane)),
        smem + vmem(3),
        moved=8 << 20,
    )
    flops = 2 * size * count * width
    expo = sds((size, count), f32)
    stat = sds((2, count), f32)
    (expo_a, stat_a), (expo_b, stat_b) = (
        call(
            functools.partial(own_kernel, slab),
            (expo, stat),
            (column, mask) + slabs,
            flops=flops,
            moved=6 << 20,
        )
        for slab, slabs in enumerate(((points,), (first, second)))
    )
    expo_c, expo_d, stat_c, stat_d, both = call(
        rest_kernel,
        (expo, expo, stat, stat, sds((2, count), f32)),
        (place, beyond, points, first, second, mask, stat_a, stat_b),
        smem + vmem(7),
        flops=2 * flops,
        moved=12 << 20,
    )
    pool = ("xl",) + narrow
    copies = jnp.broadcast_to(both, (2 * parts, 2, count))
    shared = lax.all_to_all(copies, pool, 0, 0, tiled=True)

    def sums(expo_a, expo_b, stat_a, stat_b):
        return call(
            sums_kernel,
            sds((size, padded), bf16),
            (place, expo_a, expo_b, stat_a, stat_b, shared, points, first, second),
            smem + vmem(8),
            flops=2 * flops,
            moved=10 << 20,
            scratch=[pltpu.VMEM((2, 1, count), f32)],
        )

    away = lax.ppermute(sums(expo_c, expo_d, stat_c, stat_d), across, outer)
    kept = sums(expo_a, expo_b, stat_a, stat_b)
    deep = ("zh", "zl")
    group = sds((size // 4, padded), bf16)
    cuts = call(
        cross_kernel,
        (group,) * 4,
        (place, kept, away),
        smem + vmem(2),
        scratch=[pltpu.VMEM((size, padded), bf16)],
    )
    got = [cuts[0]] + [
        lax.ppermute(cuts[k], deep, [(i, (i + near[k]) % zs) for i in range(zs)]) for k in (1, 2, 3)
    ]
    summed = call(near_kernel, group, tuple(got))
    got = lax.all_to_all(summed.reshape(4, rows, padded), "zh", 0, 0, tiled=True)
    table = call(last_kernel, sds((parts, rows, padded), bf16), (got, own))
    whole = lax.all_to_all(table, narrow, 0, 0, tiled=True)
    new_table, masses = call(
        out_kernel, (sds((parts * rows, width), f32), sds((1, parts * rows), f32)), (whole,)
    )
    return new_table, masses[0]


def solution(mesh):
    chips = Mesh(mesh.devices.reshape(4, 4, 2, 2, 4, 2), ("zh", "zl", "xh", "xl", "y", "c"))
    wide = ("zh", "zl", "xh", "xl")
    return jax.shard_map(
        shards,
        mesh=chips,
        in_specs=(P(wide, None), P(wide), P(), P(), P(wide, None)),
        out_specs=(P(wide, None), P(wide)),
        check_vma=False,
    )
```

```python
import functools

import jax
import jax.numpy as jnp
from jax import lax
from jax.experimental import pallas as pl
from jax.experimental.pallas import tpu as pltpu
from jax.sharding import Mesh, PartitionSpec as P

temper = 0.1
prior = 0.01
gone = -3e38
near = (0, 1, 2, -1)
f32 = jnp.float32
bf16 = jnp.bfloat16
i32 = jnp.int32
lane = 128


def vmem(n):
    return [pl.BlockSpec(memory_space=pltpu.VMEM)] * n


def params():
    return pltpu.CompilerParams(vmem_limit_bytes=20 * 1024 * 1024)


def mask_kernel(place_ref, lists_ref, owner_ref, *refs):
    *other, mask_ref = refs
    n, me, zl = place_ref[1], place_ref[2], place_ref[4]
    count = lists_ref.shape[1]
    blocks = owner_ref.shape[0]
    in_block = lax.broadcasted_iota(i32, (lane, count), 0)
    of_blocks = lax.broadcasted_iota(i32, (blocks, count), 0)
    of_lists = lax.broadcasted_iota(i32, lists_ref.shape, 0)
    cluster = other[0][0:1, 0:1].astype(f32).astype(i32) if other else place_ref[0]
    ids = jnp.sum(jnp.where(of_lists == cluster, lists_ref[...], 0), axis=0, keepdims=True)
    which = (of_blocks == (ids >> 7)).astype(bf16)
    here = in_block == (ids & 127)
    rows = owner_ref[...]

    def pick(table):
        found = lax.dot_general(
            table.astype(f32).astype(bf16),
            which,
            (((0,), (0,)), ((), ())),
            preferred_element_type=f32,
        )
        return jnp.sum(jnp.where(here, found, 0.0), axis=0, keepdims=True).astype(i32)

    owner = pick(rows >> 7)
    inner = pick(rows & 127)
    row = ((owner >> 1) & 1) * 64 + (owner >> 4) * 16 + (inner & 15)
    mine = ((inner >> 4) == n) & ((owner & 1) == me)
    block = jnp.where(mine, ((owner >> 2) - zl) & 3, lane)
    left = (in_block == row).astype(bf16)
    right = (in_block == block).astype(bf16)
    mask_ref[...] = lax.dot_general(
        left, right, (((1,), (1,)), ((), ())), preferred_element_type=f32
    )


def cut_kernel(place_ref, points_ref, half_ref, id_ref, sem, id_sem):
    rows = points_ref.shape[0] // 2
    start = pl.multiple_of(place_ref[3] * rows, rows)
    copy = pltpu.make_async_copy(points_ref.at[pl.ds(start, rows)], half_ref.at[pl.ds(0, rows)], sem)
    copy.start()
    id_ref[...] = jnp.full(id_ref.shape, place_ref[0].astype(f32), f32).astype(bf16)
    last = pltpu.make_async_copy(id_ref, half_ref.at[pl.ds(rows, 16)], id_sem)
    last.start()
    last.wait()
    copy.wait()


def squares(means):
    wide = means.astype(f32)
    return jnp.sum(wide * wide, axis=1, keepdims=True) * (-1.0 / temper)


def listed_rows(mask_ref, first, rows):
    picked = [mask_ref[:, first + i : first + i + 1] for i in range(rows // lane)]
    return jnp.concatenate(picked) > 0.5


def scored(means, points, bias, listed):
    dots = lax.dot_general(
        means, points, (((1,), (1,)), ((), ())), preferred_element_type=f32
    )
    t = jnp.where(listed, dots * (2.0 / temper) + bias, gone)
    top = jnp.max(t, axis=0, keepdims=True)
    expo = jnp.exp(t - top)
    return expo, top, jnp.sum(expo, axis=0, keepdims=True)


def blocks_of(count, *refs):
    step = 256
    rows = count // len(refs)
    for c in range(count // step):
        start = c * step
        ref = refs[start // rows]
        start %= rows
        yield slice(c * step, (c + 1) * step), ref, slice(start, start + step)


def score_kernel(*refs):
    *pieces, mask_ref, points_ref, expo_ref, stat_ref = refs
    means = jnp.concatenate([piece[...] for piece in pieces])
    bias = squares(means)
    listed = listed_rows(mask_ref, 0, means.shape[0])
    for at, ref, rows in blocks_of(expo_ref.shape[1], points_ref):
        expo_ref[:, at], stat_ref[0:1, at], stat_ref[1:2, at] = scored(
            means, ref[rows, :], bias, listed
        )


def other_kernel(place_ref, old_ref, *refs):
    *pieces, mask_ref, first_ref, second_ref, expo_ref, stat_ref, both_ref = refs
    means = jnp.concatenate([piece[...] for piece in pieces])
    bias = squares(means)
    listed = listed_rows(mask_ref, 0, means.shape[0])
    me, core = place_ref[2], place_ref[3]
    count = expo_ref.shape[1]
    half = count // 2
    both_ref[pl.ds(me, 1), :] = old_ref[0:1, :] + jnp.log(old_ref[1:2, :])
    for at, ref, rows in blocks_of(count, first_ref, second_ref):
        expo_ref[:, at], top, total = scored(means, ref[rows, :], bias, listed)
        stat_ref[0:1, at] = top
        stat_ref[1:2, at] = total
        start = pl.multiple_of(at.start + (half * core if at.start < half else -half * core), lane)
        both_ref[pl.ds(1 - me, 1), pl.ds(start, 256)] = top + jnp.log(total)


def sums_kernel(
    groups,
    place_ref,
    all_ref,
    points_ref,
    first_ref,
    second_ref,
    expo_a,
    stat_a,
    expo_b,
    stat_b,
    one_ref,
    two_ref,
    norm_ref,
):
    me, core = place_ref[2], place_ref[3]
    half = points_ref.shape[0] // 2
    width = points_ref.shape[1]
    for slab, which in enumerate((me, 1 - me)):
        each = [all_ref[k, pl.ds(which, 1), :] for k in range(all_ref.shape[0])]
        top = functools.reduce(jnp.maximum, each)
        total = functools.reduce(jnp.add, [jnp.exp(one - top) for one in each])
        norm_ref[slab] = top + jnp.log(total)

    def shares(expo, stat, lanes, norm):
        scale = jnp.exp(stat[0:1, lanes] - norm)
        rows = [expo[j * lane : (j + 1) * lane, lanes] for j in groups]
        return jnp.concatenate([(row * scale).astype(bf16) for row in rows])

    parts = [shares(expo_a, stat_a, slice(None), norm_ref[0])]
    for h in range(2):
        from_ = pl.ds(pl.multiple_of((core if h == 0 else 1 - core) * half, lane), half)
        at = slice(h * half, (h + 1) * half)
        parts.append(shares(expo_b, stat_b, at, norm_ref[1, :, from_]))
    step = 256
    for c in range(width // step):
        at = slice(c * step, (c + 1) * step)
        total = None
        for part, ref in zip(parts, (points_ref, first_ref, second_ref)):
            more = jnp.dot(part, ref[: part.shape[1], at], preferred_element_type=f32)
            total = more if total is None else total + more
        total = total.astype(bf16)
        one_ref[:, at] = total[:lane]
        two_ref[:, at] = total[lane:]
    mass = sum(jnp.sum(part.astype(f32), axis=1, keepdims=True) for part in parts)
    tail = halves(mass)
    one_ref[:, width:] = tail[:lane]
    two_ref[:, width:] = tail[lane:]


def added(pieces, width):
    total = pieces[0].astype(f32)
    for piece in pieces[1:]:
        total = total + piece.astype(f32)
    return total[:, :width], total[:, width : width + 1] + total[:, width + 1 : width + 2]


def halves(mass):
    high = mass.astype(bf16).astype(f32)
    lanes = lax.broadcasted_iota(i32, (mass.shape[0], lane), 1)
    return jnp.where(lanes == 0, high, jnp.where(lanes == 1, mass - high, 0.0)).astype(bf16)


def near_kernel(a, b, c, d, out):
    width = a.shape[1] - lane
    total, mass = added([a[...], b[...], c[...], d[...]], width)
    out[:, :width] = total.astype(bf16)
    out[:, width:] = halves(mass)


def last_kernel(ref, cen, out):
    width = cen.shape[1]
    total, mass = added([ref[k] for k in range(ref.shape[0])], width)
    new = (total + prior * cen[...].astype(f32)) / (mass + prior)
    new = new.astype(bf16)
    tail = halves(mass)
    for k in range(out.shape[0]):
        out[k, :, :width] = new
        out[k, :, width:] = tail


def out_kernel(ref, table_ref, mass_ref):
    parts, rows, padded = ref.shape
    width = padded - lane
    tails = []
    for k in range(parts):
        table_ref[k * rows : (k + 1) * rows, :] = ref[k, :, :width].astype(f32)
        tails.append(ref[k, :, width:].astype(f32))
    tail = jnp.concatenate(tails).T
    mass_ref[...] = tail[0:1, :] + tail[1:2, :]


def call(kernel, outs, args, specs=None, flops=0, moved=0, scratch=(), home=pltpu.VMEM):
    return pl.pallas_call(
        kernel,
        out_shape=outs,
        in_specs=specs or vmem(len(args)),
        out_specs=jax.tree.map(lambda _: pl.BlockSpec(memory_space=home), outs),
        scratch_shapes=scratch,
        compiler_params=params(),
        cost_estimate=pl.CostEstimate(flops=flops, bytes_accessed=moved, transcendentals=0),
    )(*args)


def shards(points, coarse_ids, lists, owner_map, centroids):
    narrow, deep, far = ("y", "c"), ("zh", "zl"), ("xh", "zh")
    parts, zs, peers = (lax.axis_size(a) for a in (narrow, deep, far))
    n = lax.axis_index(narrow)
    count, width = points.shape
    rows = centroids.shape[0] // parts
    size = rows * peers
    padded = width + lane
    sds = jax.ShapeDtypeStruct
    smem = [pl.BlockSpec(memory_space=pltpu.SMEM)]
    swap = [(0, 1), (1, 0)]

    def along(a, by):
        return lax.ppermute(a, deep, [(i, (i + by) % zs) for i in range(zs)])

    place = jnp.stack(
        [coarse_ids[0], n, lax.axis_index("xl"), lax.axis_index("c"), lax.axis_index("zl")]
    ).astype(i32)
    half = call(
        cut_kernel,
        sds((count // 2 + 16, width), bf16),
        (place, points),
        smem + [pl.BlockSpec(memory_space=pltpu.HBM)],
        moved=3 << 20,
        scratch=[
            pltpu.VMEM((16, width), bf16),
            pltpu.SemaphoreType.DMA,
            pltpu.SemaphoreType.DMA,
        ],
        home=pl.ANY,
    )
    first = lax.ppermute(half, "xl", swap)
    own = lax.dynamic_slice(centroids, (n * rows, 0), (rows, width))
    copies = jnp.broadcast_to(own, (peers, rows, width))
    group = lax.all_to_all(copies, far, 0, 0, tiled=True).reshape(size, width)
    pieces = [group] + [along(group, -d) for d in near[1:]]
    first, *pieces = lax.optimization_barrier((first, *pieces))
    second = lax.ppermute(first, "c", swap)
    flops = 2 * len(near) * size * count * width
    stat = sds((2, count), f32)
    expo = sds((len(near) * size, count), f32)

    def listed(*other):
        return call(
            mask_kernel,
            sds((lane, lane), f32),
            (place, lists, owner_map.reshape(-1, lane)) + other,
            smem + vmem(2 + len(other)),
            moved=8 << 20,
        )

    expo_a, stat_a = call(
        score_kernel, (expo, stat), (*pieces, listed(), points), flops=flops, moved=6 << 20
    )
    mask = listed(first[count // 2 :, :lane])
    expo_b, stat_b, both = call(
        other_kernel,
        (expo, stat, sds((2, count), f32)),
        (place, stat_a, *pieces, mask, first, second),
        smem + vmem(8),
        flops=flops,
        moved=6 << 20,
    )
    pool = ("xl",) + narrow
    copies = jnp.broadcast_to(both, (2 * parts, 2, count))
    shared = lax.all_to_all(copies, pool, 0, 0, tiled=True)

    def sums(*groups):
        return call(
            functools.partial(sums_kernel, groups),
            (sds((size, padded), bf16),) * 2,
            (place, shared, points, first, second, expo_a, stat_a, expo_b, stat_b),
            smem + vmem(8),
            flops=flops,
            moved=10 << 20,
            scratch=[pltpu.VMEM((2, 1, count), f32)],
        )

    two, one = sums(2, 1)
    three, kept = sums(3, 0)
    got = [kept, along(one, near[1]), along(two, near[2]), along(three, near[3])]
    summed = call(near_kernel, sds((size, padded), bf16), tuple(got))
    got = lax.all_to_all(summed.reshape(peers, rows, padded), far, 0, 0, tiled=True)
    table = call(last_kernel, sds((parts, rows, padded), bf16), (got, own))
    whole = lax.all_to_all(table, narrow, 0, 0, tiled=True)
    new_table, masses = call(
        out_kernel, (sds((parts * rows, width), f32), sds((1, parts * rows), f32)), (whole,)
    )
    return new_table, masses[0]


def solution(mesh):
    chips = Mesh(mesh.devices.reshape(4, 4, 2, 2, 4, 2), ("zh", "zl", "xh", "xl", "y", "c"))
    wide = ("zh", "zl", "xh", "xl")
    return jax.shard_map(
        shards,
        mesh=chips,
        in_specs=(P(wide, None), P(wide), P(), P(), P(wide, None)),
        out_specs=(P(wide, None), P(wide)),
        check_vma=False,
    )
```

```python
import functools

import jax
import jax.numpy as jnp
from jax import lax
from jax.experimental import pallas as pl
from jax.experimental.pallas import tpu as pltpu
from jax.sharding import Mesh, PartitionSpec as P

temper = 0.1
prior = 0.01
gone = -3e38
near = (0, 1, 2, -1)
f32 = jnp.float32
bf16 = jnp.bfloat16
i32 = jnp.int32
lane = 128


def vmem(n):
    return [pl.BlockSpec(memory_space=pltpu.VMEM)] * n


def params():
    return pltpu.CompilerParams(vmem_limit_bytes=20 * 1024 * 1024)


def mask_kernel(place_ref, lists_ref, owner_ref, *refs):
    *other, mask_ref = refs
    n, zl, x = place_ref[1], place_ref[4], place_ref[5]
    count = lists_ref.shape[1]
    blocks = owner_ref.shape[0]
    in_block = lax.broadcasted_iota(i32, (lane, count), 0)
    of_blocks = lax.broadcasted_iota(i32, (blocks, count), 0)
    of_lists = lax.broadcasted_iota(i32, lists_ref.shape, 0)
    cluster = other[0][0:1, 0:1].astype(f32).astype(i32) if other else place_ref[0]
    ids = jnp.sum(jnp.where(of_lists == cluster, lists_ref[...], 0), axis=0, keepdims=True)
    which = (of_blocks == (ids >> 7)).astype(bf16)
    here = in_block == (ids & 127)
    rows = owner_ref[...]

    def pick(table):
        found = lax.dot_general(
            table.astype(f32).astype(bf16),
            which,
            (((0,), (0,)), ((), ())),
            preferred_element_type=f32,
        )
        return jnp.sum(jnp.where(here, found, 0.0), axis=0, keepdims=True).astype(i32)

    owner = pick(rows >> 7)
    inner = pick(rows & 127)
    row = ((owner >> 1) & 1) * 64 + (owner >> 4) * 16 + (inner & 15)
    mine = ((inner >> 4) == n) & (((owner & 3) == x) | ((owner & 3) == 3 - x))
    block = jnp.where(mine, ((owner >> 2) - zl) & 3, lane)
    left = (in_block == row).astype(bf16)
    right = (in_block == block).astype(bf16)
    mask_ref[...] = lax.dot_general(
        left, right, (((1,), (1,)), ((), ())), preferred_element_type=f32
    )


def cut_kernel(place_ref, points_ref, half_ref, id_ref, sem, id_sem):
    rows = points_ref.shape[0] // 2
    start = pl.multiple_of(place_ref[3] * rows, rows)
    copy = pltpu.make_async_copy(points_ref.at[pl.ds(start, rows)], half_ref.at[pl.ds(0, rows)], sem)
    copy.start()
    id_ref[...] = jnp.full(id_ref.shape, place_ref[0].astype(f32), f32).astype(bf16)
    last = pltpu.make_async_copy(id_ref, half_ref.at[pl.ds(rows, 16)], id_sem)
    last.start()
    last.wait()
    copy.wait()


def squares(means):
    wide = means.astype(f32)
    return jnp.sum(wide * wide, axis=1, keepdims=True) * (-1.0 / temper)


def listed_rows(mask_ref, first, rows):
    picked = [mask_ref[:, first + i : first + i + 1] for i in range(rows // lane)]
    return jnp.concatenate(picked) > 0.5


def scored(means, points, bias, listed):
    dots = lax.dot_general(
        means, points, (((1,), (1,)), ((), ())), preferred_element_type=f32
    )
    t = jnp.where(listed, dots * (2.0 / temper) + bias, gone)
    top = jnp.max(t, axis=0, keepdims=True)
    expo = jnp.exp(t - top)
    return expo, top, jnp.sum(expo, axis=0, keepdims=True)


def blocks_of(count, *refs):
    step = 256
    rows = count // len(refs)
    for c in range(count // step):
        start = c * step
        ref = refs[start // rows]
        start %= rows
        yield slice(c * step, (c + 1) * step), ref, slice(start, start + step)


def score_kernel(*refs):
    *pieces, mask_ref, points_ref, expo_ref, stat_ref = refs
    means = jnp.concatenate([piece[...] for piece in pieces])
    bias = squares(means)
    listed = listed_rows(mask_ref, 0, means.shape[0])
    for at, ref, rows in blocks_of(expo_ref.shape[1], points_ref):
        expo_ref[:, at], stat_ref[0:1, at], stat_ref[1:2, at] = scored(
            means, ref[rows, :], bias, listed
        )


def other_kernel(place_ref, old_ref, *refs):
    *pieces, mask_ref, first_ref, second_ref, expo_ref, stat_ref, both_ref = refs
    means = jnp.concatenate([piece[...] for piece in pieces])
    bias = squares(means)
    listed = listed_rows(mask_ref, 0, means.shape[0])
    me, core = place_ref[2], place_ref[3]
    count = expo_ref.shape[1]
    half = count // 2
    both_ref[pl.ds(me, 1), :] = old_ref[0:1, :] + jnp.log(old_ref[1:2, :])
    for at, ref, rows in blocks_of(count, first_ref, second_ref):
        expo_ref[:, at], top, total = scored(means, ref[rows, :], bias, listed)
        stat_ref[0:1, at] = top
        stat_ref[1:2, at] = total
        start = pl.multiple_of(at.start + (half * core if at.start < half else -half * core), lane)
        both_ref[pl.ds(1 - me, 1), pl.ds(start, 256)] = top + jnp.log(total)


def sums_kernel(
    groups,
    place_ref,
    all_ref,
    points_ref,
    first_ref,
    second_ref,
    expo_a,
    stat_a,
    expo_b,
    stat_b,
    one_ref,
    two_ref,
    norm_ref,
):
    me, core = place_ref[2], place_ref[3]
    half = points_ref.shape[0] // 2
    width = points_ref.shape[1]
    for slab, which in enumerate((me, 1 - me)):
        each = [all_ref[k, pl.ds(which, 1), :] for k in range(all_ref.shape[0])]
        top = functools.reduce(jnp.maximum, each)
        total = functools.reduce(jnp.add, [jnp.exp(one - top) for one in each])
        norm_ref[slab] = top + jnp.log(total)

    def shares(expo, stat, lanes, norm):
        scale = jnp.exp(stat[0:1, lanes] - norm)
        rows = [expo[j * lane : (j + 1) * lane, lanes] for j in groups]
        return jnp.concatenate([(row * scale).astype(bf16) for row in rows])

    parts = [shares(expo_a, stat_a, slice(None), norm_ref[0])]
    for h in range(2):
        from_ = pl.ds(pl.multiple_of((core if h == 0 else 1 - core) * half, lane), half)
        at = slice(h * half, (h + 1) * half)
        parts.append(shares(expo_b, stat_b, at, norm_ref[1, :, from_]))
    step = 256
    for c in range(width // step):
        at = slice(c * step, (c + 1) * step)
        total = None
        for part, ref in zip(parts, (points_ref, first_ref, second_ref)):
            more = jnp.dot(part, ref[: part.shape[1], at], preferred_element_type=f32)
            total = more if total is None else total + more
        total = total.astype(bf16)
        one_ref[:, at] = total[:lane]
        two_ref[:, at] = total[lane:]
    mass = sum(jnp.sum(part.astype(f32), axis=1, keepdims=True) for part in parts)
    tail = halves(mass)
    one_ref[:, width:] = tail[:lane]
    two_ref[:, width:] = tail[lane:]


def added(pieces, width):
    total = pieces[0].astype(f32)
    for piece in pieces[1:]:
        total = total + piece.astype(f32)
    return total[:, :width], total[:, width : width + 1] + total[:, width + 1 : width + 2]


def halves(mass):
    high = mass.astype(bf16).astype(f32)
    lanes = lax.broadcasted_iota(i32, (mass.shape[0], lane), 1)
    return jnp.where(lanes == 0, high, jnp.where(lanes == 1, mass - high, 0.0)).astype(bf16)


def near_kernel(a, b, c, d, out):
    width = a.shape[1] - lane
    total, mass = added([a[...], b[...], c[...], d[...]], width)
    out[:, :width] = total.astype(bf16)
    out[:, width:] = halves(mass)


def last_kernel(ref, cen, out):
    width = cen.shape[1]
    total, mass = added([ref[k] for k in range(ref.shape[0])], width)
    new = (total + prior * cen[...].astype(f32)) / (mass + prior)
    new = new.astype(bf16)
    tail = halves(mass)
    for k in range(out.shape[0]):
        out[k, :, :width] = new
        out[k, :, width:] = tail


def out_kernel(ref, table_ref, mass_ref):
    parts, rows, padded = ref.shape
    width = padded - lane
    tails = []
    for k in range(parts):
        table_ref[k * rows : (k + 1) * rows, :] = ref[k, :, :width].astype(f32)
        tails.append(ref[k, :, width:].astype(f32))
    tail = jnp.concatenate(tails).T
    mass_ref[...] = tail[0:1, :] + tail[1:2, :]


def call(kernel, outs, args, specs=None, flops=0, moved=0, scratch=(), home=pltpu.VMEM):
    return pl.pallas_call(
        kernel,
        out_shape=outs,
        in_specs=specs or vmem(len(args)),
        out_specs=jax.tree.map(lambda _: pl.BlockSpec(memory_space=home), outs),
        scratch_shapes=scratch,
        compiler_params=params(),
        cost_estimate=pl.CostEstimate(flops=flops, bytes_accessed=moved, transcendentals=0),
    )(*args)


def shards(points, coarse_ids, lists, owner_map, centroids):
    narrow, deep, far = ("y", "c"), ("zh", "zl"), ("zh", "xh", "xl")
    parts, zs = lax.axis_size(narrow), lax.axis_size(deep)
    teams = [[4 * zh + x for x in pair for zh in range(4)] for pair in ((0, 3), (1, 2))]
    peers = len(teams[0])
    n = lax.axis_index(narrow)
    count, width = points.shape
    rows = centroids.shape[0] // parts
    size = rows * peers
    padded = width + lane
    sds = jax.ShapeDtypeStruct
    smem = [pl.BlockSpec(memory_space=pltpu.SMEM)]
    swap = [(0, 1), (1, 0)]

    def along(a, by):
        return lax.ppermute(a, deep, [(i, (i + by) % zs) for i in range(zs)])

    def team_exchange(a):
        return lax.all_to_all(a, far, 0, 0, axis_index_groups=teams, tiled=True)

    where = [lax.axis_index(a) for a in ("xl", "c", "zl", ("xh", "xl"))]
    place = jnp.stack([coarse_ids[0], n, *where]).astype(i32)
    half = call(
        cut_kernel,
        sds((count // 2 + 16, width), bf16),
        (place, points),
        smem + [pl.BlockSpec(memory_space=pltpu.HBM)],
        moved=3 << 20,
        scratch=[
            pltpu.VMEM((16, width), bf16),
            pltpu.SemaphoreType.DMA,
            pltpu.SemaphoreType.DMA,
        ],
        home=pl.ANY,
    )
    first = lax.ppermute(half, "xl", swap)
    own = lax.dynamic_slice(centroids, (n * rows, 0), (rows, width))
    copies = jnp.broadcast_to(own, (peers, rows, width))
    group = team_exchange(copies).reshape(size, width)
    pieces = [group] + [along(group, -d) for d in near[1:]]
    flops = 2 * len(near) * size * count * width
    stat = sds((2, count), f32)
    expo = sds((len(near) * size, count), f32)

    def listed(*other):
        return call(
            mask_kernel,
            sds((lane, lane), f32),
            (place, lists, owner_map.reshape(-1, lane)) + other,
            smem + vmem(2 + len(other)),
            moved=8 << 20,
        )

    first, mask, *pieces = lax.optimization_barrier((first, listed(), *pieces))
    second = lax.ppermute(first, "c", swap)
    expo_a, stat_a = call(
        score_kernel, (expo, stat), (*pieces, mask, points), flops=flops, moved=6 << 20
    )
    mask = listed(first[count // 2 :, :lane])
    expo_b, stat_b, both = call(
        other_kernel,
        (expo, stat, sds((2, count), f32)),
        (place, stat_a, *pieces, mask, first, second),
        smem + vmem(8),
        flops=flops,
        moved=6 << 20,
    )
    pool = ("xl",) + narrow
    copies = jnp.broadcast_to(both, (2 * parts, 2, count))
    shared = lax.all_to_all(copies, pool, 0, 0, tiled=True)

    def sums(*groups):
        return call(
            functools.partial(sums_kernel, groups),
            (sds((size, padded), bf16),) * 2,
            (place, shared, points, first, second, expo_a, stat_a, expo_b, stat_b),
            smem + vmem(8),
            flops=flops,
            moved=10 << 20,
            scratch=[pltpu.VMEM((2, 1, count), f32)],
        )

    two, one = sums(2, 1)
    three, kept = sums(3, 0)
    got = [kept, along(one, near[1]), along(two, near[2]), along(three, near[3])]
    summed = call(near_kernel, sds((size, padded), bf16), tuple(got))
    got = team_exchange(summed.reshape(peers, rows, padded))
    table = call(last_kernel, sds((parts, rows, padded), bf16), (got, own))
    whole = lax.all_to_all(table, narrow, 0, 0, tiled=True)
    new_table, masses = call(
        out_kernel, (sds((parts * rows, width), f32), sds((1, parts * rows), f32)), (whole,)
    )
    return new_table, masses[0]


def solution(mesh):
    chips = Mesh(mesh.devices.reshape(4, 4, 2, 2, 4, 2), ("zh", "zl", "xh", "xl", "y", "c"))
    wide = ("zh", "zl", "xh", "xl")
    return jax.shard_map(
        shards,
        mesh=chips,
        in_specs=(P(wide, None), P(wide), P(), P(), P(wide, None)),
        out_specs=(P(wide, None), P(wide)),
        check_vma=False,
    )
```

```python
import functools

import jax
import jax.numpy as jnp
from jax import lax
from jax.experimental import pallas as pl
from jax.experimental.pallas import tpu as pltpu
from jax.sharding import Mesh, PartitionSpec as P

temper = 0.1
prior = 0.01
gone = -3e38
near = (0, 1, 2, -1)
f32 = jnp.float32
bf16 = jnp.bfloat16
i32 = jnp.int32
lane = 128


def vmem(n):
    return [pl.BlockSpec(memory_space=pltpu.VMEM)] * n


def params():
    return pltpu.CompilerParams(vmem_limit_bytes=20 * 1024 * 1024)


def mask_kernel(place_ref, lists_ref, owner_ref, *refs):
    *other, mask_ref = refs
    n, zl, x = place_ref[1], place_ref[4], place_ref[5]
    count = lists_ref.shape[1]
    blocks = owner_ref.shape[0]
    in_block = lax.broadcasted_iota(i32, (lane, count), 0)
    of_blocks = lax.broadcasted_iota(i32, (blocks, count), 0)
    of_lists = lax.broadcasted_iota(i32, lists_ref.shape, 0)
    cluster = other[0][0:1, 0:1].astype(f32).astype(i32) if other else place_ref[0]
    ids = jnp.sum(jnp.where(of_lists == cluster, lists_ref[...], 0), axis=0, keepdims=True)
    which = (of_blocks == (ids >> 7)).astype(bf16)
    here = in_block == (ids & 127)
    rows = owner_ref[...]

    def pick(table):
        found = lax.dot_general(
            table.astype(f32).astype(bf16),
            which,
            (((0,), (0,)), ((), ())),
            preferred_element_type=f32,
        )
        return jnp.sum(jnp.where(here, found, 0.0), axis=0, keepdims=True).astype(i32)

    owner = pick(rows >> 7)
    inner = pick(rows & 127)
    row = ((owner >> 1) & 1) * 64 + (owner >> 4) * 16 + (inner & 15)
    mine = ((inner >> 4) == n) & (((owner & 3) == x) | ((owner & 3) == 3 - x))
    block = jnp.where(mine, ((owner >> 2) - zl) & 3, lane)
    left = (in_block == row).astype(bf16)
    right = (in_block == block).astype(bf16)
    mask_ref[...] = lax.dot_general(
        left, right, (((1,), (1,)), ((), ())), preferred_element_type=f32
    )


def cut_kernel(place_ref, points_ref, half_ref, id_ref, sem, id_sem):
    rows = points_ref.shape[0] // 2
    start = pl.multiple_of(place_ref[3] * rows, rows)
    copy = pltpu.make_async_copy(points_ref.at[pl.ds(start, rows)], half_ref.at[pl.ds(0, rows)], sem)
    copy.start()
    id_ref[...] = jnp.full(id_ref.shape, place_ref[0].astype(f32), f32).astype(bf16)
    last = pltpu.make_async_copy(id_ref, half_ref.at[pl.ds(rows, 16)], id_sem)
    last.start()
    last.wait()
    copy.wait()


def squares(means):
    wide = means.astype(f32)
    return jnp.sum(wide * wide, axis=1, keepdims=True) * (-1.0 / temper)


def listed_rows(mask_ref, first, rows):
    picked = [mask_ref[:, first + i : first + i + 1] for i in range(rows // lane)]
    return jnp.concatenate(picked) > 0.5


def scored(means, points, bias, listed):
    dots = lax.dot_general(
        means, points, (((1,), (1,)), ((), ())), preferred_element_type=f32
    )
    t = jnp.where(listed, dots * (2.0 / temper) + bias, gone)
    top = jnp.max(t, axis=0, keepdims=True)
    expo = jnp.exp(t - top)
    return expo, top, jnp.sum(expo, axis=0, keepdims=True)


def blocks_of(count, *refs):
    step = 256
    rows = count // len(refs)
    for c in range(count // step):
        start = c * step
        ref = refs[start // rows]
        start %= rows
        yield slice(c * step, (c + 1) * step), ref, slice(start, start + step)


def score_kernel(*refs):
    *pieces, mask_ref, points_ref, expo_ref, stat_ref = refs
    means = jnp.concatenate([piece[...] for piece in pieces])
    bias = squares(means)
    listed = listed_rows(mask_ref, 0, means.shape[0])
    for at, ref, rows in blocks_of(expo_ref.shape[1], points_ref):
        expo_ref[:, at], stat_ref[0:1, at], stat_ref[1:2, at] = scored(
            means, ref[rows, :], bias, listed
        )


def other_kernel(place_ref, old_ref, *refs):
    *pieces, mask_ref, first_ref, second_ref, expo_ref, stat_ref, both_ref = refs
    means = jnp.concatenate([piece[...] for piece in pieces])
    bias = squares(means)
    listed = listed_rows(mask_ref, 0, means.shape[0])
    me, core = place_ref[2], place_ref[3]
    count = expo_ref.shape[1]
    half = count // 2
    both_ref[pl.ds(me, 1), :] = old_ref[0:1, :] + jnp.log(old_ref[1:2, :])
    for at, ref, rows in blocks_of(count, first_ref, second_ref):
        expo_ref[:, at], top, total = scored(means, ref[rows, :], bias, listed)
        stat_ref[0:1, at] = top
        stat_ref[1:2, at] = total
        start = pl.multiple_of(at.start + (half * core if at.start < half else -half * core), lane)
        both_ref[pl.ds(1 - me, 1), pl.ds(start, 256)] = top + jnp.log(total)


def sums_kernel(
    groups,
    place_ref,
    all_ref,
    points_ref,
    first_ref,
    second_ref,
    expo_a,
    stat_a,
    expo_b,
    stat_b,
    *refs,
):
    *out_refs, norm_ref = refs
    me, core = place_ref[2], place_ref[3]
    half = points_ref.shape[0] // 2
    width = points_ref.shape[1]
    for slab, which in enumerate((me, 1 - me)):
        each = [all_ref[k, pl.ds(which, 1), :] for k in range(all_ref.shape[0])]
        top = functools.reduce(jnp.maximum, each)
        total = functools.reduce(jnp.add, [jnp.exp(one - top) for one in each])
        norm_ref[slab] = top + jnp.log(total)

    def shares(expo, stat, lanes, norm):
        scale = jnp.exp(stat[0:1, lanes] - norm)
        rows = [expo[j * lane : (j + 1) * lane, lanes] for j in groups]
        return jnp.concatenate([(row * scale).astype(bf16) for row in rows])

    parts = [shares(expo_a, stat_a, slice(None), norm_ref[0])]
    for h in range(2):
        from_ = pl.ds(pl.multiple_of((core if h == 0 else 1 - core) * half, lane), half)
        at = slice(h * half, (h + 1) * half)
        parts.append(shares(expo_b, stat_b, at, norm_ref[1, :, from_]))
    step = 256
    for c in range(width // step):
        at = slice(c * step, (c + 1) * step)
        total = None
        for part, ref in zip(parts, (points_ref, first_ref, second_ref)):
            more = jnp.dot(part, ref[: part.shape[1], at], preferred_element_type=f32)
            total = more if total is None else total + more
        total = total.astype(bf16)
        for k, out_ref in enumerate(out_refs):
            out_ref[:, at] = total[k * lane : (k + 1) * lane]
    mass = sum(jnp.sum(part.astype(f32), axis=1, keepdims=True) for part in parts)
    tail = halves(mass)
    for k, out_ref in enumerate(out_refs):
        out_ref[:, width:] = tail[k * lane : (k + 1) * lane]


def added(pieces, width):
    total = pieces[0].astype(f32)
    for piece in pieces[1:]:
        total = total + piece.astype(f32)
    return total[:, :width], total[:, width : width + 1] + total[:, width + 1 : width + 2]


def halves(mass):
    high = mass.astype(bf16).astype(f32)
    lanes = lax.broadcasted_iota(i32, (mass.shape[0], lane), 1)
    return jnp.where(lanes == 0, high, jnp.where(lanes == 1, mass - high, 0.0)).astype(bf16)


def near_kernel(a, b, c, d, out):
    width = a.shape[1] - lane
    total, mass = added([a[...], b[...], c[...], d[...]], width)
    out[:, :width] = total.astype(bf16)
    out[:, width:] = halves(mass)


def last_kernel(ref, cen, out):
    width = cen.shape[1]
    total, mass = added([ref[k] for k in range(ref.shape[0])], width)
    new = (total + prior * cen[...].astype(f32)) / (mass + prior)
    new = new.astype(bf16)
    tail = halves(mass)
    for k in range(out.shape[0]):
        out[k, :, :width] = new
        out[k, :, width:] = tail


def out_kernel(ref, table_ref, mass_ref):
    parts, rows, padded = ref.shape
    width = padded - lane
    tails = []
    for k in range(parts):
        table_ref[k * rows : (k + 1) * rows, :] = ref[k, :, :width].astype(f32)
        tails.append(ref[k, :, width:].astype(f32))
    tail = jnp.concatenate(tails).T
    mass_ref[...] = tail[0:1, :] + tail[1:2, :]


def call(kernel, outs, args, specs=None, flops=0, moved=0, scratch=(), home=pltpu.VMEM):
    return pl.pallas_call(
        kernel,
        out_shape=outs,
        in_specs=specs or vmem(len(args)),
        out_specs=jax.tree.map(lambda _: pl.BlockSpec(memory_space=home), outs),
        scratch_shapes=scratch,
        compiler_params=params(),
        cost_estimate=pl.CostEstimate(flops=flops, bytes_accessed=moved, transcendentals=0),
    )(*args)


def shards(points, coarse_ids, lists, owner_map, centroids):
    narrow, deep, far = ("y", "c"), ("zh", "zl"), ("zh", "xh", "xl")
    parts, zs = lax.axis_size(narrow), lax.axis_size(deep)
    teams = [[4 * zh + x for x in pair for zh in range(4)] for pair in ((0, 3), (1, 2))]
    peers = len(teams[0])
    n = lax.axis_index(narrow)
    count, width = points.shape
    rows = centroids.shape[0] // parts
    size = rows * peers
    padded = width + lane
    sds = jax.ShapeDtypeStruct
    smem = [pl.BlockSpec(memory_space=pltpu.SMEM)]
    swap = [(0, 1), (1, 0)]

    def along(a, by):
        return lax.ppermute(a, deep, [(i, (i + by) % zs) for i in range(zs)])

    def team_exchange(a):
        return lax.all_to_all(a, far, 0, 0, axis_index_groups=teams, tiled=True)

    where = [lax.axis_index(a) for a in ("xl", "c", "zl", ("xh", "xl"))]
    place = jnp.stack([coarse_ids[0], n, *where]).astype(i32)
    half = call(
        cut_kernel,
        sds((count // 2 + 16, width), bf16),
        (place, points),
        smem + [pl.BlockSpec(memory_space=pltpu.HBM)],
        moved=3 << 20,
        scratch=[
            pltpu.VMEM((16, width), bf16),
            pltpu.SemaphoreType.DMA,
            pltpu.SemaphoreType.DMA,
        ],
        home=pl.ANY,
    )
    first = lax.ppermute(half, "xl", swap)
    own = lax.dynamic_slice(centroids, (n * rows, 0), (rows, width))
    copies = jnp.broadcast_to(own, (peers, rows, width))
    group = team_exchange(copies).reshape(size, width)
    first, group = lax.optimization_barrier((first, group))
    second = lax.ppermute(first, "c", swap)
    pieces = [group] + [along(group, -d) for d in near[1:]]
    flops = 2 * len(near) * size * count * width
    stat = sds((2, count), f32)
    expo = sds((len(near) * size, count), f32)

    def listed(*other):
        return call(
            mask_kernel,
            sds((lane, lane), f32),
            (place, lists, owner_map.reshape(-1, lane)) + other,
            smem + vmem(2 + len(other)),
            moved=8 << 20,
        )

    mask = listed()
    expo_a, stat_a = call(
        score_kernel, (expo, stat), (*pieces, mask, points), flops=flops, moved=6 << 20
    )
    mask = listed(first[count // 2 :, :lane])
    expo_b, stat_b, both = call(
        other_kernel,
        (expo, stat, sds((2, count), f32)),
        (place, stat_a, *pieces, mask, first, second),
        smem + vmem(8),
        flops=flops,
        moved=6 << 20,
    )
    pool = ("xl",) + narrow
    copies = jnp.broadcast_to(both, (2 * parts, 2, count))
    shared = lax.all_to_all(copies, pool, 0, 0, tiled=True)

    def sums(*groups):
        return call(
            functools.partial(sums_kernel, groups),
            (sds((size, padded), bf16),) * len(groups),
            (place, shared, points, first, second, expo_a, stat_a, expo_b, stat_b),
            smem + vmem(8),
            flops=flops,
            moved=10 << 20,
            scratch=[pltpu.VMEM((2, 1, count), f32)],
        )

    two, one, three = sums(2, 1, 3)
    (kept,) = sums(0)
    got = [kept, along(one, near[1]), along(two, near[2]), along(three, near[3])]
    summed = call(near_kernel, sds((size, padded), bf16), tuple(got))
    got = team_exchange(summed.reshape(peers, rows, padded))
    table = call(last_kernel, sds((parts, rows, padded), bf16), (got, own))
    whole = lax.all_to_all(table, narrow, 0, 0, tiled=True)
    new_table, masses = call(
        out_kernel, (sds((parts * rows, width), f32), sds((1, parts * rows), f32)), (whole,)
    )
    return new_table, masses[0]


def solution(mesh):
    chips = Mesh(mesh.devices.reshape(4, 4, 2, 2, 4, 2), ("zh", "zl", "xh", "xl", "y", "c"))
    wide = ("zh", "zl", "xh", "xl")
    return jax.shard_map(
        shards,
        mesh=chips,
        in_specs=(P(wide, None), P(wide), P(), P(), P(wide, None)),
        out_specs=(P(wide, None), P(wide)),
        check_vma=False,
    )
```

```python
import functools

import jax
import jax.numpy as jnp
from jax import lax
from jax.experimental import pallas as pl
from jax.experimental.pallas import tpu as pltpu
from jax.sharding import Mesh, PartitionSpec as P

temper = 0.1
prior = 0.01
gone = -3e38
f32 = jnp.float32
bf16 = jnp.bfloat16
i32 = jnp.int32
lane = 128


def vmem(n):
    return [pl.BlockSpec(memory_space=pltpu.VMEM)] * n


def params():
    return pltpu.CompilerParams(vmem_limit_bytes=20 * 1024 * 1024)


def mask_kernel(place_ref, lists_ref, owner_ref, *refs):
    *other, mask_ref = refs
    n, zl, x = place_ref[1], place_ref[4], place_ref[5]
    count = lists_ref.shape[1]
    blocks = owner_ref.shape[0]
    in_block = lax.broadcasted_iota(i32, (lane, count), 0)
    of_blocks = lax.broadcasted_iota(i32, (blocks, count), 0)
    of_lists = lax.broadcasted_iota(i32, lists_ref.shape, 0)
    cluster = other[0][0:1, 0:1].astype(f32).astype(i32) if other else place_ref[0]
    ids = jnp.sum(jnp.where(of_lists == cluster, lists_ref[...], 0), axis=0, keepdims=True)
    which = (of_blocks == (ids >> 7)).astype(bf16)
    here = in_block == (ids & 127)
    rows = owner_ref[...]

    def pick(table):
        found = lax.dot_general(
            table.astype(f32).astype(bf16),
            which,
            (((0,), (0,)), ((), ())),
            preferred_element_type=f32,
        )
        return jnp.sum(jnp.where(here, found, 0.0), axis=0, keepdims=True).astype(i32)

    owner = pick(rows >> 7)
    inner = pick(rows & 127)
    row = ((owner >> 1) & 1) * 64 + (owner >> 4) * 16 + (inner & 15)
    mine = ((inner >> 4) == n) & (((owner & 3) == x) | ((owner & 3) == 3 - x))
    block = jnp.where(mine, ((owner >> 2) - zl) & 3, lane)
    left = (in_block == row).astype(bf16)
    right = (in_block == block).astype(bf16)
    mask_ref[...] = lax.dot_general(
        left, right, (((1,), (1,)), ((), ())), preferred_element_type=f32
    )


def cut_kernel(place_ref, points_ref, half_ref, id_ref, sem, id_sem):
    rows = points_ref.shape[0] // 2
    start = pl.multiple_of(place_ref[3] * rows, rows)
    copy = pltpu.make_async_copy(points_ref.at[pl.ds(start, rows)], half_ref.at[pl.ds(0, rows)], sem)
    copy.start()
    id_ref[...] = jnp.full(id_ref.shape, place_ref[0].astype(f32), f32).astype(bf16)
    last = pltpu.make_async_copy(id_ref, half_ref.at[pl.ds(rows, 16)], id_sem)
    last.start()
    last.wait()
    copy.wait()


def squares(means):
    wide = means.astype(f32)
    return jnp.sum(wide * wide, axis=1, keepdims=True) * (-1.0 / temper)


def listed_rows(mask_ref, first, rows):
    picked = [mask_ref[:, first + i : first + i + 1] for i in range(rows // lane)]
    return jnp.concatenate(picked) > 0.5


def scored(means, points, bias, listed):
    dots = lax.dot_general(
        means, points, (((1,), (1,)), ((), ())), preferred_element_type=f32
    )
    t = jnp.where(listed, dots * (2.0 / temper) + bias, gone)
    top = jnp.max(t, axis=0, keepdims=True)
    expo = jnp.exp(t - top)
    return expo, top, jnp.sum(expo, axis=0, keepdims=True)


def blocks_of(count, *refs):
    step = 256
    rows = count // len(refs)
    for c in range(count // step):
        start = c * step
        ref = refs[start // rows]
        start %= rows
        yield slice(c * step, (c + 1) * step), ref, slice(start, start + step)


def score_kernel(*refs):
    *pieces, mask_ref, points_ref, expo_ref, stat_ref = refs
    means = jnp.concatenate([piece[...] for piece in pieces])
    bias = squares(means)
    listed = listed_rows(mask_ref, 0, means.shape[0])
    for at, ref, rows in blocks_of(expo_ref.shape[1], points_ref):
        expo_ref[:, at], stat_ref[0:1, at], stat_ref[1:2, at] = scored(
            means, ref[rows, :], bias, listed
        )


def other_kernel(place_ref, old_ref, *refs):
    *pieces, mask_ref, first_ref, second_ref, expo_ref, stat_ref, both_ref = refs
    means = jnp.concatenate([piece[...] for piece in pieces])
    bias = squares(means)
    listed = listed_rows(mask_ref, 0, means.shape[0])
    me, core = place_ref[2], place_ref[3]
    count = expo_ref.shape[1]
    half = count // 2
    both_ref[pl.ds(me, 1), :] = old_ref[0:1, :] + jnp.log(old_ref[1:2, :])
    for at, ref, rows in blocks_of(count, first_ref, second_ref):
        expo_ref[:, at], top, total = scored(means, ref[rows, :], bias, listed)
        stat_ref[0:1, at] = top
        stat_ref[1:2, at] = total
        start = pl.multiple_of(at.start + (half * core if at.start < half else -half * core), lane)
        both_ref[pl.ds(1 - me, 1), pl.ds(start, 256)] = top + jnp.log(total)


def sums_kernel(
    groups,
    place_ref,
    all_ref,
    points_ref,
    first_ref,
    second_ref,
    expo_a,
    stat_a,
    expo_b,
    stat_b,
    *refs,
):
    *out_refs, norm_ref = refs
    me, core = place_ref[2], place_ref[3]
    half = points_ref.shape[0] // 2
    width = points_ref.shape[1]
    for slab, which in enumerate((me, 1 - me)):
        each = [all_ref[k, pl.ds(which, 1), :] for k in range(all_ref.shape[0])]
        top = functools.reduce(jnp.maximum, each)
        total = functools.reduce(jnp.add, [jnp.exp(one - top) for one in each])
        norm_ref[slab] = top + jnp.log(total)

    def shares(expo, stat, lanes, norm):
        scale = jnp.exp(stat[0:1, lanes] - norm)
        rows = [expo[j * lane : (j + 1) * lane, lanes] for j in groups]
        return jnp.concatenate([(row * scale).astype(bf16) for row in rows])

    parts = [shares(expo_a, stat_a, slice(None), norm_ref[0])]
    for h in range(2):
        from_ = pl.ds(pl.multiple_of((core if h == 0 else 1 - core) * half, lane), half)
        at = slice(h * half, (h + 1) * half)
        parts.append(shares(expo_b, stat_b, at, norm_ref[1, :, from_]))
    step = 256
    for c in range(width // step):
        at = slice(c * step, (c + 1) * step)
        total = None
        for part, ref in zip(parts, (points_ref, first_ref, second_ref)):
            more = jnp.dot(part, ref[: part.shape[1], at], preferred_element_type=f32)
            total = more if total is None else total + more
        total = total.astype(bf16)
        base = 0
        for out_ref in out_refs:
            out_ref[:, at] = total[base : base + out_ref.shape[0]]
            base += out_ref.shape[0]
    mass = sum(jnp.sum(part.astype(f32), axis=1, keepdims=True) for part in parts)
    tail = halves(mass)
    base = 0
    for out_ref in out_refs:
        out_ref[:, width:] = tail[base : base + out_ref.shape[0]]
        base += out_ref.shape[0]


def added(pieces, width):
    total = pieces[0].astype(f32)
    for piece in pieces[1:]:
        total = total + piece.astype(f32)
    return total[:, :width], total[:, width : width + 1] + total[:, width + 1 : width + 2]


def halves(mass):
    high = mass.astype(bf16).astype(f32)
    lanes = lax.broadcasted_iota(i32, (mass.shape[0], lane), 1)
    return jnp.where(lanes == 0, high, jnp.where(lanes == 1, mass - high, 0.0)).astype(bf16)


def near_kernel(a, low, high, b, c, out):
    width = a.shape[1] - lane
    pair = jnp.concatenate([low[...], high[...]])
    total, mass = added([a[...], pair, b[...], c[...]], width)
    out[:, :width] = total.astype(bf16)
    out[:, width:] = halves(mass)


def last_kernel(ref, cen, out):
    width = cen.shape[1]
    total, mass = added([ref[k] for k in range(ref.shape[0])], width)
    new = (total + prior * cen[...].astype(f32)) / (mass + prior)
    new = new.astype(bf16)
    tail = halves(mass)
    for k in range(out.shape[0]):
        out[k, :, :width] = new
        out[k, :, width:] = tail


def out_kernel(ref, table_ref, mass_ref):
    parts, rows, padded = ref.shape
    width = padded - lane
    tails = []
    for k in range(parts):
        table_ref[k * rows : (k + 1) * rows, :] = ref[k, :, :width].astype(f32)
        tails.append(ref[k, :, width:].astype(f32))
    tail = jnp.concatenate(tails).T
    mass_ref[...] = tail[0:1, :] + tail[1:2, :]


def call(kernel, outs, args, specs=None, flops=0, moved=0, scratch=(), home=pltpu.VMEM):
    return pl.pallas_call(
        kernel,
        out_shape=outs,
        in_specs=specs or vmem(len(args)),
        out_specs=jax.tree.map(lambda _: pl.BlockSpec(memory_space=home), outs),
        scratch_shapes=scratch,
        compiler_params=params(),
        cost_estimate=pl.CostEstimate(flops=flops, bytes_accessed=moved, transcendentals=0),
    )(*args)


def shards(points, coarse_ids, lists, owner_map, centroids):
    narrow, deep, far = ("y", "c"), ("zh", "zl"), ("zh", "xh", "xl")
    parts, zs = lax.axis_size(narrow), lax.axis_size(deep)
    teams = [[4 * zh + x for x in pair for zh in range(4)] for pair in ((0, 3), (1, 2))]
    peers = len(teams[0])
    n = lax.axis_index(narrow)
    count, width = points.shape
    rows = centroids.shape[0] // parts
    size = rows * peers
    padded = width + lane
    sds = jax.ShapeDtypeStruct
    smem = [pl.BlockSpec(memory_space=pltpu.SMEM)]
    swap = [(0, 1), (1, 0)]

    def along(a, by):
        return lax.ppermute(a, deep, [(i, (i + by) % zs) for i in range(zs)])

    def team_exchange(a):
        return lax.all_to_all(a, far, 0, 0, axis_index_groups=teams, tiled=True)

    where = [lax.axis_index(a) for a in ("xl", "c", "zl", ("xh", "xl"))]
    place = jnp.stack([coarse_ids[0], n, *where]).astype(i32)
    half = call(
        cut_kernel,
        sds((count // 2 + 16, width), bf16),
        (place, points),
        smem + [pl.BlockSpec(memory_space=pltpu.HBM)],
        moved=3 << 20,
        scratch=[
            pltpu.VMEM((16, width), bf16),
            pltpu.SemaphoreType.DMA,
            pltpu.SemaphoreType.DMA,
        ],
        home=pl.ANY,
    )
    first = lax.ppermute(half, "xl", swap)
    own = lax.dynamic_slice(centroids, (n * rows, 0), (rows, width))
    copies = jnp.broadcast_to(own, (peers, rows, width))
    group = team_exchange(copies).reshape(size, width)
    middle = size // 2
    two = [along(group[:middle], -2), along(group[middle:], 2)]
    pieces = [group, along(group, -1), *two, along(group, 1)]
    flops = 2 * 4 * size * count * width
    stat = sds((2, count), f32)
    expo = sds((4 * size, count), f32)

    def listed(*other):
        return call(
            mask_kernel,
            sds((lane, lane), f32),
            (place, lists, owner_map.reshape(-1, lane)) + other,
            smem + vmem(2 + len(other)),
            moved=8 << 20,
        )

    first, mask, *pieces = lax.optimization_barrier((first, listed(), *pieces))
    second = lax.ppermute(first, "c", swap)
    expo_a, stat_a = call(
        score_kernel, (expo, stat), (*pieces, mask, points), flops=flops, moved=6 << 20
    )
    mask = listed(first[count // 2 :, :lane])
    expo_b, stat_b, both = call(
        other_kernel,
        (expo, stat, sds((2, count), f32)),
        (place, stat_a, *pieces, mask, first, second),
        smem + vmem(4 + len(pieces)),
        flops=flops,
        moved=6 << 20,
    )
    pool = ("xl",) + narrow
    copies = jnp.broadcast_to(both, (2 * parts, 2, count))
    shared = lax.all_to_all(copies, pool, 0, 0, tiled=True)

    def sums(groups, cuts):
        return call(
            functools.partial(sums_kernel, groups),
            tuple(sds((cut, padded), bf16) for cut in cuts),
            (place, shared, points, first, second, expo_a, stat_a, expo_b, stat_b),
            smem + vmem(8),
            flops=flops,
            moved=10 << 20,
            scratch=[pltpu.VMEM((2, 1, count), f32)],
        )

    low, high, one, three = sums((2, 1, 3), (size // 2, size // 2, size, size))
    (kept,) = sums((0,), (size,))
    got = [kept, along(low, 2), along(high, -2), along(one, 1), along(three, -1)]
    summed = call(near_kernel, sds((size, padded), bf16), tuple(got))
    got = team_exchange(summed.reshape(peers, rows, padded))
    table = call(last_kernel, sds((parts, rows, padded), bf16), (got, own))
    whole = lax.all_to_all(table, narrow, 0, 0, tiled=True)
    new_table, masses = call(
        out_kernel, (sds((parts * rows, width), f32), sds((1, parts * rows), f32)), (whole,)
    )
    return new_table, masses[0]


def solution(mesh):
    chips = Mesh(mesh.devices.reshape(4, 4, 2, 2, 4, 2), ("zh", "zl", "xh", "xl", "y", "c"))
    wide = ("zh", "zl", "xh", "xl")
    return jax.shard_map(
        shards,
        mesh=chips,
        in_specs=(P(wide, None), P(wide), P(), P(), P(wide, None)),
        out_specs=(P(wide, None), P(wide)),
        check_vma=False,
    )
```

```python
import functools

import jax
import jax.numpy as jnp
from jax import lax
from jax.experimental import pallas as pl
from jax.experimental.pallas import tpu as pltpu
from jax.sharding import Mesh, PartitionSpec as P

temper = 0.1
prior = 0.01
gone = -3e38
f32 = jnp.float32
bf16 = jnp.bfloat16
i32 = jnp.int32
lane = 128


def vmem(n):
    return [pl.BlockSpec(memory_space=pltpu.VMEM)] * n


def params():
    return pltpu.CompilerParams(vmem_limit_bytes=20 * 1024 * 1024)


def mask_kernel(place_ref, lists_ref, owner_ref, *refs):
    if len(refs) == 1:
        (mask_ref,) = refs
        cluster = place_ref[0]
    else:
        other_ref, mask_ref, keep_ref = refs
        kept = keep_ref.shape[0]
        keep_ref[...] = other_ref[:kept, :]
        cluster = other_ref[kept : kept + 16, :lane].astype(f32)[0:1, 0:1].astype(i32)
    n, zl, x = place_ref[1], place_ref[4], place_ref[5]
    count = lists_ref.shape[1]
    blocks = owner_ref.shape[0]
    in_block = lax.broadcasted_iota(i32, (lane, count), 0)
    of_blocks = lax.broadcasted_iota(i32, (blocks, count), 0)
    of_lists = lax.broadcasted_iota(i32, lists_ref.shape, 0)
    ids = jnp.sum(jnp.where(of_lists == cluster, lists_ref[...], 0), axis=0, keepdims=True)
    which = (of_blocks == (ids >> 7)).astype(bf16)
    here = in_block == (ids & 127)
    rows = owner_ref[...]

    def pick(table):
        found = lax.dot_general(
            table.astype(f32).astype(bf16),
            which,
            (((0,), (0,)), ((), ())),
            preferred_element_type=f32,
        )
        return jnp.sum(jnp.where(here, found, 0.0), axis=0, keepdims=True).astype(i32)

    owner = pick(rows >> 7)
    inner = pick(rows & 127)
    row = ((owner >> 1) & 1) * 64 + (owner >> 4) * 16 + (inner & 15)
    mine = ((inner >> 4) == n) & (((owner & 3) == x) | ((owner & 3) == 3 - x))
    block = jnp.where(mine, ((owner >> 2) - zl) & 3, lane)
    left = (in_block == row).astype(bf16)
    right = (in_block == block).astype(bf16)
    mask_ref[...] = lax.dot_general(
        left, right, (((1,), (1,)), ((), ())), preferred_element_type=f32
    )


def cut_kernel(place_ref, points_ref, half_ref, id_ref, sem, id_sem):
    rows = points_ref.shape[0] // 2
    start = pl.multiple_of(place_ref[3] * rows, rows)
    copy = pltpu.make_async_copy(points_ref.at[pl.ds(start, rows)], half_ref.at[pl.ds(0, rows)], sem)
    copy.start()
    id_ref[...] = jnp.full(id_ref.shape, place_ref[0].astype(f32), f32).astype(bf16)
    last = pltpu.make_async_copy(id_ref, half_ref.at[pl.ds(rows, 16)], id_sem)
    last.start()
    last.wait()
    copy.wait()


def squares(means):
    wide = means.astype(f32)
    return jnp.sum(wide * wide, axis=1, keepdims=True) * (-1.0 / temper)


def listed_rows(mask_ref, first, rows):
    picked = [mask_ref[:, first + i : first + i + 1] for i in range(rows // lane)]
    return jnp.concatenate(picked) > 0.5


def scored(means, points, bias, listed):
    dots = lax.dot_general(
        means, points, (((1,), (1,)), ((), ())), preferred_element_type=f32
    )
    t = jnp.where(listed, dots * (2.0 / temper) + bias, gone)
    top = jnp.max(t, axis=0, keepdims=True)
    expo = jnp.exp(t - top)
    return expo, top, jnp.sum(expo, axis=0, keepdims=True)


def blocks_of(count, *refs):
    step = 256
    rows = count // len(refs)
    for c in range(count // step):
        start = c * step
        ref = refs[start // rows]
        start %= rows
        yield slice(c * step, (c + 1) * step), ref, slice(start, start + step)


def score_kernel(*refs):
    *pieces, mask_ref, points_ref, expo_ref, stat_ref = refs
    means = jnp.concatenate([piece[...] for piece in pieces])
    bias = squares(means)
    listed = listed_rows(mask_ref, 0, means.shape[0])
    for at, ref, rows in blocks_of(expo_ref.shape[1], points_ref):
        expo_ref[:, at], stat_ref[0:1, at], stat_ref[1:2, at] = scored(
            means, ref[rows, :], bias, listed
        )


def other_kernel(place_ref, old_ref, *refs):
    *pieces, mask_ref, first_ref, second_ref, expo_ref, stat_ref, both_ref = refs
    means = jnp.concatenate([piece[...] for piece in pieces])
    bias = squares(means)
    listed = listed_rows(mask_ref, 0, means.shape[0])
    me, core = place_ref[2], place_ref[3]
    count = expo_ref.shape[1]
    half = count // 2
    both_ref[pl.ds(me, 1), :] = old_ref[0:1, :] + jnp.log(old_ref[1:2, :])
    for at, ref, rows in blocks_of(count, first_ref, second_ref):
        expo_ref[:, at], top, total = scored(means, ref[rows, :], bias, listed)
        stat_ref[0:1, at] = top
        stat_ref[1:2, at] = total
        start = pl.multiple_of(at.start + (half * core if at.start < half else -half * core), lane)
        both_ref[pl.ds(1 - me, 1), pl.ds(start, 256)] = top + jnp.log(total)


def sums_kernel(
    groups,
    place_ref,
    all_ref,
    points_ref,
    first_ref,
    second_ref,
    expo_a,
    stat_a,
    expo_b,
    stat_b,
    *refs,
):
    *out_refs, norm_ref = refs
    me, core = place_ref[2], place_ref[3]
    half = points_ref.shape[0] // 2
    width = points_ref.shape[1]
    for slab, which in enumerate((me, 1 - me)):
        each = [all_ref[k, pl.ds(which, 1), :] for k in range(all_ref.shape[0])]
        top = functools.reduce(jnp.maximum, each)
        total = functools.reduce(jnp.add, [jnp.exp(one - top) for one in each])
        norm_ref[slab] = top + jnp.log(total)

    def shares(expo, stat, lanes, norm):
        scale = jnp.exp(stat[0:1, lanes] - norm)
        rows = [expo[j * lane : (j + 1) * lane, lanes] for j in groups]
        return jnp.concatenate([(row * scale).astype(bf16) for row in rows])

    parts = [shares(expo_a, stat_a, slice(None), norm_ref[0])]
    for h in range(2):
        from_ = pl.ds(pl.multiple_of((core if h == 0 else 1 - core) * half, lane), half)
        at = slice(h * half, (h + 1) * half)
        parts.append(shares(expo_b, stat_b, at, norm_ref[1, :, from_]))
    step = 256
    for c in range(width // step):
        at = slice(c * step, (c + 1) * step)
        total = None
        for part, ref in zip(parts, (points_ref, first_ref, second_ref)):
            more = jnp.dot(part, ref[: part.shape[1], at], preferred_element_type=f32)
            total = more if total is None else total + more
        total = total.astype(bf16)
        base = 0
        for out_ref in out_refs:
            out_ref[:, at] = total[base : base + out_ref.shape[0]]
            base += out_ref.shape[0]
    mass = sum(jnp.sum(part.astype(f32), axis=1, keepdims=True) for part in parts)
    tail = halves(mass)
    base = 0
    for out_ref in out_refs:
        out_ref[:, width:] = tail[base : base + out_ref.shape[0]]
        base += out_ref.shape[0]


def added(pieces, width):
    total = pieces[0].astype(f32)
    for piece in pieces[1:]:
        total = total + piece.astype(f32)
    return total[:, :width], total[:, width : width + 1] + total[:, width + 1 : width + 2]


def halves(mass):
    high = mass.astype(bf16).astype(f32)
    lanes = lax.broadcasted_iota(i32, (mass.shape[0], lane), 1)
    return jnp.where(lanes == 0, high, jnp.where(lanes == 1, mass - high, 0.0)).astype(bf16)


def near_kernel(a, low, high, b, c, out):
    width = a.shape[1] - lane
    pair = jnp.concatenate([low[...], high[...]])
    total, mass = added([a[...], pair, b[...], c[...]], width)
    out[:, :width] = total.astype(bf16)
    out[:, width:] = halves(mass)


def last_kernel(ref, cen, out):
    width = cen.shape[1]
    total, mass = added([ref[k] for k in range(ref.shape[0])], width)
    new = (total + prior * cen[...].astype(f32)) / (mass + prior)
    new = new.astype(bf16)
    tail = halves(mass)
    for k in range(out.shape[0]):
        out[k, :, :width] = new
        out[k, :, width:] = tail


def out_kernel(ref, table_ref, mass_ref):
    parts, rows, padded = ref.shape
    width = padded - lane
    tails = []
    for k in range(parts):
        table_ref[k * rows : (k + 1) * rows, :] = ref[k, :, :width].astype(f32)
        tails.append(ref[k, :, width:].astype(f32))
    tail = jnp.concatenate(tails).T
    mass_ref[...] = tail[0:1, :] + tail[1:2, :]


def call(kernel, outs, args, specs=None, flops=0, moved=0, scratch=(), home=pltpu.VMEM):
    return pl.pallas_call(
        kernel,
        out_shape=outs,
        in_specs=specs or vmem(len(args)),
        out_specs=jax.tree.map(lambda _: pl.BlockSpec(memory_space=home), outs),
        scratch_shapes=scratch,
        compiler_params=params(),
        cost_estimate=pl.CostEstimate(flops=flops, bytes_accessed=moved, transcendentals=0),
    )(*args)


def shards(points, coarse_ids, lists, owner_map, centroids):
    narrow, deep, far = ("y", "c"), ("zh", "zl"), ("zh", "xh", "xl")
    parts, zs = lax.axis_size(narrow), lax.axis_size(deep)
    teams = [[4 * zh + x for x in pair for zh in range(4)] for pair in ((0, 3), (1, 2))]
    peers = len(teams[0])
    n = lax.axis_index(narrow)
    count, width = points.shape
    rows = centroids.shape[0] // parts
    size = rows * peers
    padded = width + lane
    sds = jax.ShapeDtypeStruct
    smem = [pl.BlockSpec(memory_space=pltpu.SMEM)]
    swap = [(0, 1), (1, 0)]

    def along(a, by):
        return lax.ppermute(a, deep, [(i, (i + by) % zs) for i in range(zs)])

    def team_exchange(a):
        return lax.all_to_all(a, far, 0, 0, axis_index_groups=teams, tiled=True)

    where = [lax.axis_index(a) for a in ("xl", "c", "zl", ("xh", "xl"))]
    place = jnp.stack([coarse_ids[0], n, *where]).astype(i32)
    half = call(
        cut_kernel,
        sds((count // 2 + 16, width), bf16),
        (place, points),
        smem + [pl.BlockSpec(memory_space=pltpu.HBM)],
        moved=3 << 20,
        scratch=[
            pltpu.VMEM((16, width), bf16),
            pltpu.SemaphoreType.DMA,
            pltpu.SemaphoreType.DMA,
        ],
        home=pl.ANY,
    )
    first = lax.ppermute(half, "xl", swap)
    own = lax.dynamic_slice(centroids, (n * rows, 0), (rows, width))
    copies = jnp.broadcast_to(own, (peers, rows, width))
    group = team_exchange(copies).reshape(size, width)
    middle = size // 2
    two = [along(group[:middle], -2), along(group[middle:], 2)]
    pieces = [group, along(group, -1), *two, along(group, 1)]
    flops = 2 * 4 * size * count * width
    stat = sds((2, count), f32)
    expo = sds((4 * size, count), f32)

    def listed(*other):
        return call(
            mask_kernel,
            (sds((lane, lane), f32),) + tuple(sds((count // 2, width), bf16) for _ in other),
            (place, lists, owner_map.reshape(-1, lane)) + other,
            smem + vmem(2 + len(other)),
            moved=8 << 20,
        )

    (mask,) = listed()
    mask_b, first = listed(first)
    first, mask, mask_b, *pieces = lax.optimization_barrier((first, mask, mask_b, *pieces))
    second = lax.ppermute(first, "c", swap)
    expo_a, stat_a = call(
        score_kernel, (expo, stat), (*pieces, mask, points), flops=flops, moved=6 << 20
    )
    expo_b, stat_b, both = call(
        other_kernel,
        (expo, stat, sds((2, count), f32)),
        (place, stat_a, *pieces, mask_b, first, second),
        smem + vmem(4 + len(pieces)),
        flops=flops,
        moved=6 << 20,
    )
    pool = ("xl",) + narrow
    copies = jnp.broadcast_to(both, (2 * parts, 2, count))
    shared = lax.all_to_all(copies, pool, 0, 0, tiled=True)

    def sums(groups, cuts):
        return call(
            functools.partial(sums_kernel, groups),
            tuple(sds((cut, padded), bf16) for cut in cuts),
            (place, shared, points, first, second, expo_a, stat_a, expo_b, stat_b),
            smem + vmem(8),
            flops=flops,
            moved=10 << 20,
            scratch=[pltpu.VMEM((2, 1, count), f32)],
        )

    low, high, one, three = sums((2, 1, 3), (size // 2, size // 2, size, size))
    (kept,) = sums((0,), (size,))
    got = [kept, along(low, 2), along(high, -2), along(one, 1), along(three, -1)]
    summed = call(near_kernel, sds((size, padded), bf16), tuple(got))
    got = team_exchange(summed.reshape(peers, rows, padded))
    table = call(last_kernel, sds((parts, rows, padded), bf16), (got, own))
    whole = lax.all_to_all(table, narrow, 0, 0, tiled=True)
    new_table, masses = call(
        out_kernel, (sds((parts * rows, width), f32), sds((1, parts * rows), f32)), (whole,)
    )
    return new_table, masses[0]


def solution(mesh):
    chips = Mesh(mesh.devices.reshape(4, 4, 2, 2, 4, 2), ("zh", "zl", "xh", "xl", "y", "c"))
    wide = ("zh", "zl", "xh", "xl")
    return jax.shard_map(
        shards,
        mesh=chips,
        in_specs=(P(wide, None), P(wide), P(), P(), P(wide, None)),
        out_specs=(P(wide, None), P(wide)),
        check_vma=False,
    )
```

```python
import functools

import jax
import jax.numpy as jnp
from jax import lax
from jax.experimental import pallas as pl
from jax.experimental.pallas import tpu as pltpu
from jax.sharding import Mesh, PartitionSpec as P

temper = 0.1
prior = 0.01
gone = -3e38
f32 = jnp.float32
bf16 = jnp.bfloat16
i32 = jnp.int32
lane = 128


def vmem(n):
    return [pl.BlockSpec(memory_space=pltpu.VMEM)] * n


def params():
    return pltpu.CompilerParams(vmem_limit_bytes=20 * 1024 * 1024)


def mask_kernel(place_ref, lists_ref, owner_ref, *refs):
    if len(refs) == 1:
        (mask_ref,) = refs
        cluster = place_ref[0]
    else:
        other_ref, mask_ref, keep_ref = refs
        kept = keep_ref.shape[0]
        keep_ref[...] = other_ref[:kept, :]
        cluster = other_ref[kept : kept + 16, :lane].astype(f32)[0:1, 0:1].astype(i32)
    n, zl, x = place_ref[1], place_ref[4], place_ref[5]
    count = lists_ref.shape[1]
    blocks = owner_ref.shape[0]
    in_block = lax.broadcasted_iota(i32, (lane, count), 0)
    of_blocks = lax.broadcasted_iota(i32, (blocks, count), 0)
    of_lists = lax.broadcasted_iota(i32, lists_ref.shape, 0)
    ids = jnp.sum(jnp.where(of_lists == cluster, lists_ref[...], 0), axis=0, keepdims=True)
    which = (of_blocks == (ids >> 7)).astype(bf16)
    here = in_block == (ids & 127)
    rows = owner_ref[...]

    def pick(table):
        found = lax.dot_general(
            table.astype(f32).astype(bf16),
            which,
            (((0,), (0,)), ((), ())),
            preferred_element_type=f32,
        )
        return jnp.sum(jnp.where(here, found, 0.0), axis=0, keepdims=True).astype(i32)

    owner = pick(rows >> 7)
    inner = pick(rows & 127)
    row = ((owner >> 1) & 1) * 64 + (owner >> 4) * 16 + (inner & 15)
    mine = ((inner >> 4) == n) & (((owner & 3) == x) | ((owner & 3) == 3 - x))
    block = jnp.where(mine, ((owner >> 2) - zl) & 3, lane)
    left = (in_block == row).astype(bf16)
    right = (in_block == block).astype(bf16)
    mask_ref[...] = lax.dot_general(
        left, right, (((1,), (1,)), ((), ())), preferred_element_type=f32
    )


def cut_kernel(place_ref, points_ref, half_ref, id_ref, sem, id_sem):
    rows = points_ref.shape[0] // 2
    start = pl.multiple_of(place_ref[3] * rows, rows)
    copy = pltpu.make_async_copy(points_ref.at[pl.ds(start, rows)], half_ref.at[pl.ds(0, rows)], sem)
    copy.start()
    id_ref[...] = jnp.full(id_ref.shape, place_ref[0].astype(f32), f32).astype(bf16)
    last = pltpu.make_async_copy(id_ref, half_ref.at[pl.ds(rows, 16)], id_sem)
    last.start()
    last.wait()
    copy.wait()


def squares(means):
    wide = means.astype(f32)
    return jnp.sum(wide * wide, axis=1, keepdims=True) * (-1.0 / temper)


def listed_rows(mask_ref, first, rows):
    picked = [mask_ref[:, first + i : first + i + 1] for i in range(rows // lane)]
    return jnp.concatenate(picked) > 0.5


def scored(means, points, bias, listed):
    dots = lax.dot_general(
        means, points, (((1,), (1,)), ((), ())), preferred_element_type=f32
    )
    t = jnp.where(listed, dots * (2.0 / temper) + bias, gone)
    top = jnp.max(t, axis=0, keepdims=True)
    expo = jnp.exp(t - top)
    return expo, top, jnp.sum(expo, axis=0, keepdims=True)


def blocks_of(count, *refs):
    step = 256
    rows = count // len(refs)
    for c in range(count // step):
        start = c * step
        ref = refs[start // rows]
        start %= rows
        yield slice(c * step, (c + 1) * step), ref, slice(start, start + step)


def score_kernel(*refs):
    *pieces, mask_ref, points_ref, expo_ref, stat_ref = refs
    means = jnp.concatenate([piece[...] for piece in pieces])
    bias = squares(means)
    listed = listed_rows(mask_ref, 0, means.shape[0])
    for at, ref, rows in blocks_of(expo_ref.shape[1], points_ref):
        expo_ref[:, at], stat_ref[0:1, at], stat_ref[1:2, at] = scored(
            means, ref[rows, :], bias, listed
        )


def other_kernel(place_ref, old_ref, *refs):
    *pieces, mask_ref, first_ref, second_ref, expo_ref, stat_ref, both_ref = refs
    means = jnp.concatenate([piece[...] for piece in pieces])
    bias = squares(means)
    listed = listed_rows(mask_ref, 0, means.shape[0])
    me, core = place_ref[2], place_ref[3]
    count = expo_ref.shape[1]
    half = count // 2
    both_ref[pl.ds(me, 1), :] = old_ref[0:1, :] + jnp.log(old_ref[1:2, :])
    for at, ref, rows in blocks_of(count, first_ref, second_ref):
        expo_ref[:, at], top, total = scored(means, ref[rows, :], bias, listed)
        stat_ref[0:1, at] = top
        stat_ref[1:2, at] = total
        start = pl.multiple_of(at.start + (half * core if at.start < half else -half * core), lane)
        both_ref[pl.ds(1 - me, 1), pl.ds(start, 256)] = top + jnp.log(total)


def sums_kernel(
    groups,
    place_ref,
    all_ref,
    points_ref,
    first_ref,
    second_ref,
    expo_a,
    stat_a,
    expo_b,
    stat_b,
    *refs,
):
    *out_refs, norm_ref = refs
    me, core = place_ref[2], place_ref[3]
    half = points_ref.shape[0] // 2
    width = points_ref.shape[1]
    for slab, which in enumerate((me, 1 - me)):
        each = [all_ref[k, pl.ds(which, 1), :] for k in range(all_ref.shape[0])]
        top = functools.reduce(jnp.maximum, each)
        total = functools.reduce(jnp.add, [jnp.exp(one - top) for one in each])
        norm_ref[slab] = top + jnp.log(total)

    def shares(expo, stat, lanes, norm):
        scale = jnp.exp(stat[0:1, lanes] - norm)
        rows = [expo[j * lane : (j + 1) * lane, lanes] for j in groups]
        return jnp.concatenate([(row * scale).astype(bf16) for row in rows])

    parts = [shares(expo_a, stat_a, slice(None), norm_ref[0])]
    for h in range(2):
        from_ = pl.ds(pl.multiple_of((core if h == 0 else 1 - core) * half, lane), half)
        at = slice(h * half, (h + 1) * half)
        parts.append(shares(expo_b, stat_b, at, norm_ref[1, :, from_]))
    step = 256
    for c in range(width // step):
        at = slice(c * step, (c + 1) * step)
        total = None
        for part, ref in zip(parts, (points_ref, first_ref, second_ref)):
            more = jnp.dot(part, ref[: part.shape[1], at], preferred_element_type=f32)
            total = more if total is None else total + more
        total = total.astype(bf16)
        base = 0
        for out_ref in out_refs:
            out_ref[:, at] = total[base : base + out_ref.shape[0]]
            base += out_ref.shape[0]
    mass = sum(jnp.sum(part.astype(f32), axis=1, keepdims=True) for part in parts)
    tail = halves(mass)
    base = 0
    for out_ref in out_refs:
        out_ref[:, width:] = tail[base : base + out_ref.shape[0]]
        base += out_ref.shape[0]


def added(pieces, width):
    total = pieces[0].astype(f32)
    for piece in pieces[1:]:
        total = total + piece.astype(f32)
    return total[:, :width], total[:, width : width + 1] + total[:, width + 1 : width + 2]


def halves(mass):
    high = mass.astype(bf16).astype(f32)
    lanes = lax.broadcasted_iota(i32, (mass.shape[0], lane), 1)
    return jnp.where(lanes == 0, high, jnp.where(lanes == 1, mass - high, 0.0)).astype(bf16)


def near_kernel(a, low, high, b, c, out):
    width = a.shape[1] - lane
    pair = jnp.concatenate([low[...], high[...]])
    total, mass = added([a[...], pair, b[...], c[...]], width)
    out[:, :width] = total.astype(bf16)
    out[:, width:] = halves(mass)


def last_kernel(ref, cen, out):
    width = cen.shape[1]
    total, mass = added([ref[k] for k in range(ref.shape[0])], width)
    new = (total + prior * cen[...].astype(f32)) / (mass + prior)
    new = new.astype(bf16)
    tail = halves(mass)
    for k in range(out.shape[0]):
        out[k, :, :width] = new
        out[k, :, width:] = tail


def out_kernel(ref, table_ref, mass_ref):
    parts, rows, padded = ref.shape
    width = padded - lane
    tails = []
    for k in range(parts):
        table_ref[k * rows : (k + 1) * rows, :] = ref[k, :, :width].astype(f32)
        tails.append(ref[k, :, width:].astype(f32))
    tail = jnp.concatenate(tails).T
    mass_ref[...] = tail[0:1, :] + tail[1:2, :]


def call(kernel, outs, args, specs=None, flops=0, moved=0, scratch=(), home=pltpu.VMEM):
    return pl.pallas_call(
        kernel,
        out_shape=outs,
        in_specs=specs or vmem(len(args)),
        out_specs=jax.tree.map(lambda _: pl.BlockSpec(memory_space=home), outs),
        scratch_shapes=scratch,
        compiler_params=params(),
        cost_estimate=pl.CostEstimate(flops=flops, bytes_accessed=moved, transcendentals=0),
    )(*args)


def shards(points, coarse_ids, lists, owner_map, centroids):
    narrow, deep, far = ("y", "c"), ("zh", "zl"), ("zh", "xh", "xl")
    parts, zs = lax.axis_size(narrow), lax.axis_size(deep)
    teams = [[4 * zh + x for x in pair for zh in range(4)] for pair in ((0, 3), (1, 2))]
    peers = len(teams[0])
    n = lax.axis_index(narrow)
    count, width = points.shape
    rows = centroids.shape[0] // parts
    size = rows * peers
    padded = width + lane
    sds = jax.ShapeDtypeStruct
    smem = [pl.BlockSpec(memory_space=pltpu.SMEM)]
    swap = [(0, 1), (1, 0)]

    def along(a, by):
        return lax.ppermute(a, deep, [(i, (i + by) % zs) for i in range(zs)])

    def team_exchange(a):
        return lax.all_to_all(a, far, 0, 0, axis_index_groups=teams, tiled=True)

    where = [lax.axis_index(a) for a in ("xl", "c", "zl", ("xh", "xl"))]
    place = jnp.stack([coarse_ids[0], n, *where]).astype(i32)
    half = call(
        cut_kernel,
        sds((count // 2 + 16, width), bf16),
        (place, points),
        smem + [pl.BlockSpec(memory_space=pltpu.HBM)],
        moved=3 << 20,
        scratch=[
            pltpu.VMEM((16, width), bf16),
            pltpu.SemaphoreType.DMA,
            pltpu.SemaphoreType.DMA,
        ],
        home=pl.ANY,
    )
    first = lax.ppermute(half, "xl", swap)
    own = lax.dynamic_slice(centroids, (n * rows, 0), (rows, width))
    group = lax.all_gather(own, far, axis=0, axis_index_groups=teams, tiled=True)
    middle = size // 2
    two = [along(group[:middle], -2), along(group[middle:], 2)]
    pieces = [group, along(group, -1), *two, along(group, 1)]
    flops = 2 * 4 * size * count * width
    stat = sds((2, count), f32)
    expo = sds((4 * size, count), f32)

    def listed(*other):
        return call(
            mask_kernel,
            (sds((lane, lane), f32),) + tuple(sds((count // 2, width), bf16) for _ in other),
            (place, lists, owner_map.reshape(-1, lane)) + other,
            smem + vmem(2 + len(other)),
            moved=8 << 20,
        )

    (mask,) = listed()
    mask_b, first = listed(first)
    first, mask, mask_b, *pieces = lax.optimization_barrier((first, mask, mask_b, *pieces))
    second = lax.ppermute(first, "c", swap)
    expo_a, stat_a = call(
        score_kernel, (expo, stat), (*pieces, mask, points), flops=flops, moved=6 << 20
    )
    expo_b, stat_b, both = call(
        other_kernel,
        (expo, stat, sds((2, count), f32)),
        (place, stat_a, *pieces, mask_b, first, second),
        smem + vmem(4 + len(pieces)),
        flops=flops,
        moved=6 << 20,
    )
    pool = ("xl",) + narrow
    copies = jnp.broadcast_to(both, (2 * parts, 2, count))
    shared = lax.all_to_all(copies, pool, 0, 0, tiled=True)

    def sums(groups, cuts):
        return call(
            functools.partial(sums_kernel, groups),
            tuple(sds((cut, padded), bf16) for cut in cuts),
            (place, shared, points, first, second, expo_a, stat_a, expo_b, stat_b),
            smem + vmem(8),
            flops=flops,
            moved=10 << 20,
            scratch=[pltpu.VMEM((2, 1, count), f32)],
        )

    low, high, one, three = sums((2, 1, 3), (size // 2, size // 2, size, size))
    (kept,) = sums((0,), (size,))
    got = [kept, along(low, 2), along(high, -2), along(one, 1), along(three, -1)]
    summed = call(near_kernel, sds((size, padded), bf16), tuple(got))
    got = team_exchange(summed.reshape(peers, rows, padded))
    table = call(last_kernel, sds((parts, rows, padded), bf16), (got, own))
    whole = lax.all_to_all(table, narrow, 0, 0, tiled=True)
    new_table, masses = call(
        out_kernel, (sds((parts * rows, width), f32), sds((1, parts * rows), f32)), (whole,)
    )
    return new_table, masses[0]


def solution(mesh):
    chips = Mesh(mesh.devices.reshape(4, 4, 2, 2, 4, 2), ("zh", "zl", "xh", "xl", "y", "c"))
    wide = ("zh", "zl", "xh", "xl")
    return jax.shard_map(
        shards,
        mesh=chips,
        in_specs=(P(wide, None), P(wide), P(), P(), P(wide, None)),
        out_specs=(P(wide, None), P(wide)),
        check_vma=False,
    )
```

```python
import functools

import jax
import jax.numpy as jnp
from jax import lax
from jax.experimental import pallas as pl
from jax.experimental.pallas import tpu as pltpu
from jax.sharding import Mesh, PartitionSpec as P

temper = 0.1
prior = 0.01
gone = -3e38
f32 = jnp.float32
bf16 = jnp.bfloat16
i32 = jnp.int32
lane = 128


def vmem(n):
    return [pl.BlockSpec(memory_space=pltpu.VMEM)] * n


def params():
    return pltpu.CompilerParams(vmem_limit_bytes=20 * 1024 * 1024)


def mask_kernel(place_ref, lists_ref, owner_ref, *refs):
    if len(refs) == 1:
        (mask_ref,) = refs
        cluster = place_ref[0]
    else:
        other_ref, mask_ref, keep_ref = refs
        kept = keep_ref.shape[0]
        keep_ref[...] = other_ref[:kept, :]
        cluster = other_ref[kept : kept + 16, :lane].astype(f32)[0:1, 0:1].astype(i32)
    n, zl, x = place_ref[1], place_ref[4], place_ref[5]
    count = lists_ref.shape[1]
    blocks = owner_ref.shape[0]
    in_block = lax.broadcasted_iota(i32, (lane, count), 0)
    of_blocks = lax.broadcasted_iota(i32, (blocks, count), 0)
    of_lists = lax.broadcasted_iota(i32, lists_ref.shape, 0)
    ids = jnp.sum(jnp.where(of_lists == cluster, lists_ref[...], 0), axis=0, keepdims=True)
    which = (of_blocks == (ids >> 7)).astype(bf16)
    here = in_block == (ids & 127)
    rows = owner_ref[...]

    def pick(table):
        found = lax.dot_general(
            table.astype(f32).astype(bf16),
            which,
            (((0,), (0,)), ((), ())),
            preferred_element_type=f32,
        )
        return jnp.sum(jnp.where(here, found, 0.0), axis=0, keepdims=True).astype(i32)

    owner = pick(rows >> 7)
    inner = pick(rows & 127)
    row = ((owner >> 1) & 1) * 64 + (owner >> 4) * 16 + (inner & 15)
    mine = ((inner >> 4) == n) & (((owner & 3) == x) | ((owner & 3) == 3 - x))
    block = jnp.where(mine, ((owner >> 2) - zl) & 3, lane)
    left = (in_block == row).astype(bf16)
    right = (in_block == block).astype(bf16)
    mask_ref[...] = lax.dot_general(
        left, right, (((1,), (1,)), ((), ())), preferred_element_type=f32
    )


def cut_kernel(place_ref, points_ref, half_ref, id_ref, sem, id_sem):
    rows = points_ref.shape[0] // 2
    start = pl.multiple_of(place_ref[3] * rows, rows)
    copy = pltpu.make_async_copy(points_ref.at[pl.ds(start, rows)], half_ref.at[pl.ds(0, rows)], sem)
    copy.start()
    id_ref[...] = jnp.full(id_ref.shape, place_ref[0].astype(f32), f32).astype(bf16)
    last = pltpu.make_async_copy(id_ref, half_ref.at[pl.ds(rows, 16)], id_sem)
    last.start()
    last.wait()
    copy.wait()


def squares(means):
    wide = means.astype(f32)
    return jnp.sum(wide * wide, axis=1, keepdims=True) * (-1.0 / temper)


def listed_rows(mask_ref, first, rows):
    picked = [mask_ref[:, first + i : first + i + 1] for i in range(rows // lane)]
    return jnp.concatenate(picked) > 0.5


def scored(means, points, bias, listed):
    dots = lax.dot_general(
        means, points, (((1,), (1,)), ((), ())), preferred_element_type=f32
    )
    t = jnp.where(listed, dots * (2.0 / temper) + bias, gone)
    top = jnp.max(t, axis=0, keepdims=True)
    expo = jnp.exp(t - top)
    return expo, top, jnp.sum(expo, axis=0, keepdims=True)


def blocks_of(count, *refs):
    step = 256
    rows = count // len(refs)
    for c in range(count // step):
        start = c * step
        ref = refs[start // rows]
        start %= rows
        yield slice(c * step, (c + 1) * step), ref, slice(start, start + step)


def score_kernel(*refs):
    *pieces, mask_ref, points_ref, expo_ref, stat_ref = refs
    means = jnp.concatenate([piece[...] for piece in pieces])
    bias = squares(means)
    listed = listed_rows(mask_ref, 0, means.shape[0])
    for at, ref, rows in blocks_of(expo_ref.shape[1], points_ref):
        expo_ref[:, at], stat_ref[0:1, at], stat_ref[1:2, at] = scored(
            means, ref[rows, :], bias, listed
        )


def other_kernel(place_ref, old_ref, *refs):
    *pieces, mask_ref, first_ref, second_ref, expo_ref, stat_ref, both_ref = refs
    means = jnp.concatenate([piece[...] for piece in pieces])
    bias = squares(means)
    listed = listed_rows(mask_ref, 0, means.shape[0])
    me, core = place_ref[2], place_ref[3]
    count = expo_ref.shape[1]
    half = count // 2
    both_ref[pl.ds(me, 1), :] = old_ref[0:1, :] + jnp.log(old_ref[1:2, :])
    for at, ref, rows in blocks_of(count, first_ref, second_ref):
        expo_ref[:, at], top, total = scored(means, ref[rows, :], bias, listed)
        stat_ref[0:1, at] = top
        stat_ref[1:2, at] = total
        start = pl.multiple_of(at.start + (half * core if at.start < half else -half * core), lane)
        both_ref[pl.ds(1 - me, 1), pl.ds(start, 256)] = top + jnp.log(total)


def sums_kernel(
    groups,
    place_ref,
    all_ref,
    points_ref,
    first_ref,
    second_ref,
    expo_a,
    stat_a,
    expo_b,
    stat_b,
    *refs,
):
    *out_refs, norm_ref = refs
    me, core = place_ref[2], place_ref[3]
    half = points_ref.shape[0] // 2
    width = points_ref.shape[1]
    each = [all_ref[k] for k in range(all_ref.shape[0])]
    top = functools.reduce(jnp.maximum, each)
    total = functools.reduce(jnp.add, [jnp.exp(one - top) for one in each])
    norm_ref[...] = top + jnp.log(total)
    mine, theirs = pl.ds(me, 1), pl.ds(1 - me, 1)

    def shares(expo, stat, lanes, norm):
        scale = jnp.exp(stat[0:1, lanes] - norm)
        rows = [expo[j * lane : (j + 1) * lane, lanes] for j in groups]
        return jnp.concatenate([(row * scale).astype(bf16) for row in rows])

    parts = [shares(expo_a, stat_a, slice(None), norm_ref[mine, :])]
    for h in range(2):
        from_ = pl.ds(pl.multiple_of((core if h == 0 else 1 - core) * half, lane), half)
        at = slice(h * half, (h + 1) * half)
        parts.append(shares(expo_b, stat_b, at, norm_ref[theirs, from_]))
    step = 256
    for c in range(width // step):
        at = slice(c * step, (c + 1) * step)
        total = None
        for part, ref in zip(parts, (points_ref, first_ref, second_ref)):
            more = jnp.dot(part, ref[: part.shape[1], at], preferred_element_type=f32)
            total = more if total is None else total + more
        total = total.astype(bf16)
        base = 0
        for out_ref in out_refs:
            out_ref[:, at] = total[base : base + out_ref.shape[0]]
            base += out_ref.shape[0]
    mass = sum(jnp.sum(part.astype(f32), axis=1, keepdims=True) for part in parts)
    tail = halves(mass)
    base = 0
    for out_ref in out_refs:
        out_ref[:, width:] = tail[base : base + out_ref.shape[0]]
        base += out_ref.shape[0]


def added(pieces, width):
    total = pieces[0].astype(f32)
    for piece in pieces[1:]:
        total = total + piece.astype(f32)
    return total[:, :width], total[:, width : width + 1] + total[:, width + 1 : width + 2]


def halves(mass):
    high = mass.astype(bf16).astype(f32)
    lanes = lax.broadcasted_iota(i32, (mass.shape[0], lane), 1)
    return jnp.where(lanes == 0, high, jnp.where(lanes == 1, mass - high, 0.0)).astype(bf16)


def near_kernel(a, low, high, b, c, out):
    width = a.shape[1] - lane
    pair = jnp.concatenate([low[...], high[...]])
    total, mass = added([a[...], pair, b[...], c[...]], width)
    out[:, :width] = total.astype(bf16)
    out[:, width:] = halves(mass)


def last_kernel(ref, cen, out):
    width = cen.shape[1]
    total, mass = added([ref[k] for k in range(ref.shape[0])], width)
    new = (total + prior * cen[...].astype(f32)) / (mass + prior)
    new = new.astype(bf16)
    tail = halves(mass)
    for k in range(out.shape[0]):
        out[k, :, :width] = new
        out[k, :, width:] = tail


def out_kernel(ref, table_ref, mass_ref):
    parts, rows, padded = ref.shape
    width = padded - lane
    tails = []
    for k in range(parts):
        table_ref[k * rows : (k + 1) * rows, :] = ref[k, :, :width].astype(f32)
        tails.append(ref[k, :, width:].astype(f32))
    tail = jnp.concatenate(tails).T
    mass_ref[...] = tail[0:1, :] + tail[1:2, :]


def call(kernel, outs, args, specs=None, flops=0, moved=0, scratch=(), home=pltpu.VMEM):
    return pl.pallas_call(
        kernel,
        out_shape=outs,
        in_specs=specs or vmem(len(args)),
        out_specs=jax.tree.map(lambda _: pl.BlockSpec(memory_space=home), outs),
        scratch_shapes=scratch,
        compiler_params=params(),
        cost_estimate=pl.CostEstimate(flops=flops, bytes_accessed=moved, transcendentals=0),
    )(*args)


def shards(points, coarse_ids, lists, owner_map, centroids):
    narrow, deep, far = ("y", "c"), ("zh", "zl"), ("zh", "xh", "xl")
    parts, zs = lax.axis_size(narrow), lax.axis_size(deep)
    teams = [[4 * zh + x for x in pair for zh in range(4)] for pair in ((0, 3), (1, 2))]
    peers = len(teams[0])
    n = lax.axis_index(narrow)
    count, width = points.shape
    rows = centroids.shape[0] // parts
    size = rows * peers
    padded = width + lane
    sds = jax.ShapeDtypeStruct
    smem = [pl.BlockSpec(memory_space=pltpu.SMEM)]
    swap = [(0, 1), (1, 0)]

    def along(a, by):
        return lax.ppermute(a, deep, [(i, (i + by) % zs) for i in range(zs)])

    def team_exchange(a):
        return lax.all_to_all(a, far, 0, 0, axis_index_groups=teams, tiled=True)

    where = [lax.axis_index(a) for a in ("xl", "c", "zl", ("xh", "xl"))]
    place = jnp.stack([coarse_ids[0], n, *where]).astype(i32)
    half = call(
        cut_kernel,
        sds((count // 2 + 16, width), bf16),
        (place, points),
        smem + [pl.BlockSpec(memory_space=pltpu.HBM)],
        moved=3 << 20,
        scratch=[
            pltpu.VMEM((16, width), bf16),
            pltpu.SemaphoreType.DMA,
            pltpu.SemaphoreType.DMA,
        ],
        home=pl.ANY,
    )
    first = lax.ppermute(half, "xl", swap)
    own = lax.dynamic_slice(centroids, (n * rows, 0), (rows, width))
    copies = jnp.broadcast_to(own, (peers, rows, width))
    group = team_exchange(copies).reshape(size, width)
    middle = size // 2
    two = [along(group[:middle], -2), along(group[middle:], 2)]
    pieces = [group, along(group, -1), *two, along(group, 1)]
    flops = 2 * 4 * size * count * width
    stat = sds((2, count), f32)
    expo = sds((4 * size, count), f32)

    def listed(*other):
        return call(
            mask_kernel,
            (sds((lane, lane), f32),) + tuple(sds((count // 2, width), bf16) for _ in other),
            (place, lists, owner_map.reshape(-1, lane)) + other,
            smem + vmem(2 + len(other)),
            moved=8 << 20,
        )

    (mask,) = listed()
    mask_b, first = listed(first)
    first, mask, mask_b, *pieces = lax.optimization_barrier((first, mask, mask_b, *pieces))
    second = lax.ppermute(first, "c", swap)
    expo_a, stat_a = call(
        score_kernel, (expo, stat), (*pieces, mask, points), flops=flops, moved=6 << 20
    )
    expo_b, stat_b, both = call(
        other_kernel,
        (expo, stat, sds((2, count), f32)),
        (place, stat_a, *pieces, mask_b, first, second),
        smem + vmem(4 + len(pieces)),
        flops=flops,
        moved=6 << 20,
    )
    pool = ("xl",) + narrow
    copies = jnp.broadcast_to(both, (2 * parts, 2, count))
    shared = lax.all_to_all(copies, pool, 0, 0, tiled=True)

    def sums(groups, cuts):
        return call(
            functools.partial(sums_kernel, groups),
            tuple(sds((cut, padded), bf16) for cut in cuts),
            (place, shared, points, first, second, expo_a, stat_a, expo_b, stat_b),
            smem + vmem(8),
            flops=flops,
            moved=10 << 20,
            scratch=[pltpu.VMEM((2, count), f32)],
        )

    low, high, one, three = sums((2, 1, 3), (size // 2, size // 2, size, size))
    (kept,) = sums((0,), (size,))
    got = [kept, along(low, 2), along(high, -2), along(one, 1), along(three, -1)]
    summed = call(near_kernel, sds((size, padded), bf16), tuple(got))
    got = team_exchange(summed.reshape(peers, rows, padded))
    table = call(last_kernel, sds((parts, rows, padded), bf16), (got, own))
    whole = lax.all_to_all(table, narrow, 0, 0, tiled=True)
    new_table, masses = call(
        out_kernel, (sds((parts * rows, width), f32), sds((1, parts * rows), f32)), (whole,)
    )
    return new_table, masses[0]


def solution(mesh):
    chips = Mesh(mesh.devices.reshape(4, 4, 2, 2, 4, 2), ("zh", "zl", "xh", "xl", "y", "c"))
    wide = ("zh", "zl", "xh", "xl")
    return jax.shard_map(
        shards,
        mesh=chips,
        in_specs=(P(wide, None), P(wide), P(), P(), P(wide, None)),
        out_specs=(P(wide, None), P(wide)),
        check_vma=False,
    )
```

```python
import functools

import jax
import jax.numpy as jnp
from jax import lax
from jax.experimental import pallas as pl
from jax.experimental.pallas import tpu as pltpu
from jax.sharding import Mesh, PartitionSpec as P

temper = 0.1
prior = 0.01
gone = -3e38
f32 = jnp.float32
bf16 = jnp.bfloat16
i32 = jnp.int32
lane = 128


def vmem(n):
    return [pl.BlockSpec(memory_space=pltpu.VMEM)] * n


def params():
    return pltpu.CompilerParams(vmem_limit_bytes=20 * 1024 * 1024)


def mask_kernel(place_ref, lists_ref, owner_ref, *refs):
    if len(refs) == 1:
        (mask_ref,) = refs
        cluster = place_ref[0]
    else:
        other_ref, mask_ref, keep_ref = refs
        kept = keep_ref.shape[0]
        keep_ref[...] = other_ref[:kept, :]
        cluster = other_ref[kept : kept + 16, :lane].astype(f32)[0:1, 0:1].astype(i32)
    n, zl, x = place_ref[1], place_ref[4], place_ref[5]
    count = lists_ref.shape[1]
    blocks = owner_ref.shape[0]
    in_block = lax.broadcasted_iota(i32, (lane, count), 0)
    of_blocks = lax.broadcasted_iota(i32, (blocks, count), 0)
    of_lists = lax.broadcasted_iota(i32, lists_ref.shape, 0)
    ids = jnp.sum(jnp.where(of_lists == cluster, lists_ref[...], 0), axis=0, keepdims=True)
    which = (of_blocks == (ids >> 7)).astype(bf16)
    here = in_block == (ids & 127)
    rows = owner_ref[...]

    def pick(table):
        found = lax.dot_general(
            table.astype(f32).astype(bf16),
            which,
            (((0,), (0,)), ((), ())),
            preferred_element_type=f32,
        )
        return jnp.sum(jnp.where(here, found, 0.0), axis=0, keepdims=True).astype(i32)

    owner = pick(rows >> 7)
    inner = pick(rows & 127)
    row = ((owner >> 1) & 1) * 64 + (owner >> 4) * 16 + (inner & 15)
    mine = ((inner >> 4) == n) & (((owner & 3) == x) | ((owner & 3) == 3 - x))
    block = jnp.where(mine, ((owner >> 2) - zl) & 3, lane)
    left = (in_block == row).astype(bf16)
    right = (in_block == block).astype(bf16)
    mask_ref[...] = lax.dot_general(
        left, right, (((1,), (1,)), ((), ())), preferred_element_type=f32
    )


def cut_kernel(place_ref, points_ref, half_ref, id_ref, sem, id_sem):
    rows = points_ref.shape[0] // 2
    start = pl.multiple_of(place_ref[3] * rows, rows)
    copy = pltpu.make_async_copy(points_ref.at[pl.ds(start, rows)], half_ref.at[pl.ds(0, rows)], sem)
    copy.start()
    id_ref[...] = jnp.full(id_ref.shape, place_ref[0].astype(f32), f32).astype(bf16)
    last = pltpu.make_async_copy(id_ref, half_ref.at[pl.ds(rows, 16)], id_sem)
    last.start()
    last.wait()
    copy.wait()


def squares(means):
    wide = means.astype(f32)
    return jnp.sum(wide * wide, axis=1, keepdims=True) * (-1.0 / temper)


def listed_rows(mask_ref, first, rows):
    picked = [mask_ref[:, first + i : first + i + 1] for i in range(rows // lane)]
    return jnp.concatenate(picked) > 0.5


def scored(means, points, bias, listed):
    dots = lax.dot_general(
        means, points, (((1,), (1,)), ((), ())), preferred_element_type=f32
    )
    t = jnp.where(listed, dots * (2.0 / temper) + bias, gone)
    top = jnp.max(t, axis=0, keepdims=True)
    expo = jnp.exp(t - top)
    return expo, top, jnp.sum(expo, axis=0, keepdims=True)


def blocks_of(count, *refs):
    step = 256
    rows = count // len(refs)
    for c in range(count // step):
        start = c * step
        ref = refs[start // rows]
        start %= rows
        yield slice(c * step, (c + 1) * step), ref, slice(start, start + step)


def score_kernel(*refs):
    *pieces, mask_ref, points_ref, expo_ref, stat_ref = refs
    means = jnp.concatenate([piece[...] for piece in pieces])
    bias = squares(means)
    listed = listed_rows(mask_ref, 0, means.shape[0])
    for at, ref, rows in blocks_of(expo_ref.shape[1], points_ref):
        expo_ref[:, at], stat_ref[0:1, at], stat_ref[1:2, at] = scored(
            means, ref[rows, :], bias, listed
        )


def other_kernel(place_ref, old_ref, *refs):
    *pieces, mask_ref, first_ref, second_ref, expo_ref, stat_ref, both_ref = refs
    means = jnp.concatenate([piece[...] for piece in pieces])
    bias = squares(means)
    listed = listed_rows(mask_ref, 0, means.shape[0])
    me, core = place_ref[2], place_ref[3]
    count = expo_ref.shape[1]
    half = count // 2
    both_ref[pl.ds(me, 1), :] = old_ref[0:1, :] + jnp.log(old_ref[1:2, :])
    for at, ref, rows in blocks_of(count, first_ref, second_ref):
        expo_ref[:, at], top, total = scored(means, ref[rows, :], bias, listed)
        stat_ref[0:1, at] = top
        stat_ref[1:2, at] = total
        start = pl.multiple_of(at.start + (half * core if at.start < half else -half * core), lane)
        both_ref[pl.ds(1 - me, 1), pl.ds(start, 256)] = top + jnp.log(total)


def sums_kernel(
    groups,
    place_ref,
    all_ref,
    points_ref,
    first_ref,
    second_ref,
    expo_a,
    stat_a,
    expo_b,
    stat_b,
    *refs,
):
    *out_refs, norm_ref = refs
    me, core = place_ref[2], place_ref[3]
    half = points_ref.shape[0] // 2
    width = points_ref.shape[1]
    each = [all_ref[k] for k in range(all_ref.shape[0])]
    top = functools.reduce(jnp.maximum, each)
    total = functools.reduce(jnp.add, [jnp.exp(one - top) for one in each])
    norm_ref[...] = top + jnp.log(total)
    mine, theirs = pl.ds(me, 1), pl.ds(1 - me, 1)

    def shares(expo, stat, lanes, norm):
        scale = jnp.exp(stat[0:1, lanes] - norm)
        rows = [expo[j * lane : (j + 1) * lane, lanes] for j in groups]
        return jnp.concatenate([(row * scale).astype(bf16) for row in rows])

    parts = [shares(expo_a, stat_a, slice(None), norm_ref[mine, :])]
    for h in range(2):
        from_ = pl.ds(pl.multiple_of((core if h == 0 else 1 - core) * half, lane), half)
        at = slice(h * half, (h + 1) * half)
        parts.append(shares(expo_b, stat_b, at, norm_ref[theirs, from_]))
    step = 256
    for c in range(width // step):
        at = slice(c * step, (c + 1) * step)
        total = None
        for part, ref in zip(parts, (points_ref, first_ref, second_ref)):
            more = jnp.dot(part, ref[: part.shape[1], at], preferred_element_type=f32)
            total = more if total is None else total + more
        total = total.astype(bf16)
        base = 0
        for out_ref in out_refs:
            out_ref[:, at] = total[base : base + out_ref.shape[0]]
            base += out_ref.shape[0]
    mass = sum(jnp.sum(part.astype(f32), axis=1, keepdims=True) for part in parts)
    tail = halves(mass)
    base = 0
    for out_ref in out_refs:
        out_ref[:, width:] = tail[base : base + out_ref.shape[0]]
        base += out_ref.shape[0]


def added(pieces, width):
    total = pieces[0].astype(f32)
    for piece in pieces[1:]:
        total = total + piece.astype(f32)
    return total[:, :width], total[:, width : width + 1] + total[:, width + 1 : width + 2]


def halves(mass):
    high = mass.astype(bf16).astype(f32)
    lanes = lax.broadcasted_iota(i32, (mass.shape[0], lane), 1)
    return jnp.where(lanes == 0, high, jnp.where(lanes == 1, mass - high, 0.0)).astype(bf16)


def near_kernel(a, low, high, b, c, out):
    width = a.shape[1] - lane
    pair = jnp.concatenate([low[...], high[...]])
    total, mass = added([a[...], pair, b[...], c[...]], width)
    out[:, :width] = total.astype(bf16)
    out[:, width:] = halves(mass)


def last_kernel(ref, cen, out):
    width = cen.shape[1]
    total, mass = added([ref[k] for k in range(ref.shape[0])], width)
    new = (total + prior * cen[...].astype(f32)) / (mass + prior)
    new = new.astype(bf16)
    tail = halves(mass)
    for k in range(out.shape[0]):
        out[k, :, :width] = new
        out[k, :, width:] = tail


def out_kernel(ref, table_ref, mass_ref):
    parts, rows, padded = ref.shape
    width = padded - lane
    tails = []
    for k in range(parts):
        table_ref[k * rows : (k + 1) * rows, :] = ref[k, :, :width].astype(f32)
        tails.append(ref[k, :, width:].astype(f32))
    tail = jnp.concatenate(tails).T
    mass_ref[...] = tail[0:1, :] + tail[1:2, :]


def call(kernel, outs, args, specs=None, flops=0, moved=0, scratch=(), home=pltpu.VMEM):
    return pl.pallas_call(
        kernel,
        out_shape=outs,
        in_specs=specs or vmem(len(args)),
        out_specs=jax.tree.map(lambda _: pl.BlockSpec(memory_space=home), outs),
        scratch_shapes=scratch,
        compiler_params=params(),
        cost_estimate=pl.CostEstimate(flops=flops, bytes_accessed=moved, transcendentals=0),
    )(*args)


def shards(points, coarse_ids, lists, owner_map, centroids):
    narrow, deep, far = ("y", "c"), ("zh", "zl"), ("zh", "xh", "xl")
    parts, zs = lax.axis_size(narrow), lax.axis_size(deep)
    teams = [[4 * zh + x for x in pair for zh in range(4)] for pair in ((0, 3), (1, 2))]
    peers = len(teams[0])
    n = lax.axis_index(narrow)
    count, width = points.shape
    rows = centroids.shape[0] // parts
    size = rows * peers
    padded = width + lane
    sds = jax.ShapeDtypeStruct
    smem = [pl.BlockSpec(memory_space=pltpu.SMEM)]
    swap = [(0, 1), (1, 0)]

    def along(a, by):
        return lax.ppermute(a, deep, [(i, (i + by) % zs) for i in range(zs)])

    def team_exchange(a):
        return lax.all_to_all(a, far, 0, 0, axis_index_groups=teams, tiled=True)

    where = [lax.axis_index(a) for a in ("xl", "c", "zl", ("xh", "xl"))]
    place = jnp.stack([coarse_ids[0], n, *where]).astype(i32)
    half = call(
        cut_kernel,
        sds((count // 2 + 16, width), bf16),
        (place, points),
        smem + [pl.BlockSpec(memory_space=pltpu.HBM)],
        moved=3 << 20,
        scratch=[
            pltpu.VMEM((16, width), bf16),
            pltpu.SemaphoreType.DMA,
            pltpu.SemaphoreType.DMA,
        ],
        home=pl.ANY,
    )
    first = lax.ppermute(half, "xl", swap)
    own = lax.dynamic_slice(centroids, (n * rows, 0), (rows, width))
    copies = jnp.broadcast_to(own, (peers, rows, width))
    group = team_exchange(copies).reshape(size, width)
    middle = size // 2
    two = [along(group[:middle], -2), along(group[middle:], 2)]
    pieces = [group, along(group, -1), *two, along(group, 1)]
    flops = 2 * 4 * size * count * width
    stat = sds((2, count), f32)
    expo = sds((4 * size, count), f32)

    def listed(*other):
        return call(
            mask_kernel,
            (sds((lane, lane), f32),) + tuple(sds((count // 2, width), bf16) for _ in other),
            (place, lists, owner_map.reshape(-1, lane)) + other,
            smem + vmem(2 + len(other)),
            moved=8 << 20,
        )

    (mask,) = listed()
    mask_b, first = listed(first)
    first, mask, mask_b, *pieces = lax.optimization_barrier((first, mask, mask_b, *pieces))
    second = lax.ppermute(first, "c", swap)
    expo_a, stat_a = call(
        score_kernel, (expo, stat), (*pieces, mask, points), flops=flops, moved=6 << 20
    )
    expo_b, stat_b, both = call(
        other_kernel,
        (expo, stat, sds((2, count), f32)),
        (place, stat_a, *pieces, mask_b, first, second),
        smem + vmem(4 + len(pieces)),
        flops=flops,
        moved=6 << 20,
    )
    pool = ("xl",) + narrow
    copies = jnp.broadcast_to(both, (2 * parts, 2, count))
    shared = lax.all_to_all(copies, pool, 0, 0, tiled=True)

    def sums(groups, cuts):
        return call(
            functools.partial(sums_kernel, groups),
            tuple(sds((cut, padded), bf16) for cut in cuts),
            (place, shared, points, first, second, expo_a, stat_a, expo_b, stat_b),
            smem + vmem(8),
            flops=flops,
            moved=10 << 20,
            scratch=[pltpu.VMEM((2, count), f32)],
        )

    one, three = sums((1, 3), (size, size))
    low, high = sums((2,), (size // 2, size // 2))
    (kept,) = sums((0,), (size,))
    got = [kept, along(low, 2), along(high, -2), along(one, 1), along(three, -1)]
    summed = call(near_kernel, sds((size, padded), bf16), tuple(got))
    got = team_exchange(summed.reshape(peers, rows, padded))
    table = call(last_kernel, sds((parts, rows, padded), bf16), (got, own))
    whole = lax.all_to_all(table, narrow, 0, 0, tiled=True)
    new_table, masses = call(
        out_kernel, (sds((parts * rows, width), f32), sds((1, parts * rows), f32)), (whole,)
    )
    return new_table, masses[0]


def solution(mesh):
    chips = Mesh(mesh.devices.reshape(4, 4, 2, 2, 4, 2), ("zh", "zl", "xh", "xl", "y", "c"))
    wide = ("zh", "zl", "xh", "xl")
    return jax.shard_map(
        shards,
        mesh=chips,
        in_specs=(P(wide, None), P(wide), P(), P(), P(wide, None)),
        out_specs=(P(wide, None), P(wide)),
        check_vma=False,
    )
```
